32 devices in a mesh: groups: 2 (over x), seq: 8 (over z, y), head: 2 (over core).
Axes of the slice: x: 2, y: 2, z: 4, core: 2. Of those that a mesh axis runs over, the one named last changes fastest.
Arguments:
- query_proj: bfloat16 [3072, 2048], P(('groups', 'seq'), 'head'), parts along dimension 0, may hold values from -43 to 43
- key_proj: bfloat16 [3072, 2048], P(('groups', 'seq'), 'head'), parts along dimension 0, may hold values from -43 to 43
- value_proj: bfloat16 [3072, 4096], P(('groups', 'seq'), 'head'), parts along dimension 0, may hold values from -43 to 43
- gate_proj: bfloat16 [3072, 4096], P(('groups', 'seq'), 'head'), parts along dimension 0, may hold values from -6 to 6
- write_strength: float32 [3072, 32], P(('groups', 'seq'), 'head'), parts along dimension 0, may hold values from 0 to 1
- log_decay: float32 [3072, 32], P(('groups', 'seq'), 'head'), parts along dimension 0, may hold values from -2 to 0
- conv_query: bfloat16 [4, 2048], P(None, 'head'), may hold values from -3 to 3
- conv_key: bfloat16 [4, 2048], P(None, 'head'), may hold values from -3 to 3
- conv_value: bfloat16 [4, 4096], P(None, 'head'), may hold values from -3 to 3
- norm_gain: float32 [128], replicated, may hold values from 0.5 to 1.5
Outputs:
- mixer_out: bfloat16 [3072, 4096], P(('groups', 'seq'), 'head'), parts along dimension 0
The draws below stay inside these ranges and needn't reach their ends.
There are 2 independent parts, one for each index of `groups`. The reference program is written for one: setup_inputs(seed, part) draws one part's arguments, and reference() takes and returns one part's arrays. A program takes and returns all parts, laid end to end along the dimension named above; an argument that names none is the same for every part. Nothing has to cross between parts.
All inputs are finite; a program needn't handle non-finite values.
Results may differ from the reference program's by a relative error of at most 0.0075.
Values may be sent and summed in bfloat16 or wider, within the bound.
A program may use at most 128 MiB of HBM per device.

```python
import math
import jax
import jax.numpy as jnp
from jax import lax

KH = 16
VALUE_HEADS = 32
DK = 128
DV = 128
CONV = 4
SPAN = 64
SEQUENCE_LENGTH = 1536
KDIM = 2048
VDIM = 4096


def spread_rows(key, row_count, col_count):
    col_scale = jnp.exp(jax.random.uniform(jax.random.fold_in(key, 1), (1, col_count), jnp.float32, -1.2, 1.2))
    row_scale = jnp.exp(jax.random.uniform(jax.random.fold_in(key, 2), (row_count, 1), jnp.float32, -1.15, 1.15))
    base = jnp.clip(jax.random.normal(jax.random.fold_in(key, 4), (row_count, col_count), jnp.float32), -4.0, 4.0)
    return (base * col_scale * row_scale).astype(jnp.bfloat16)


def draw_query_proj(key, part):
    return spread_rows(jax.random.fold_in(key, 11), SEQUENCE_LENGTH, KDIM)


def draw_key_proj(key, part):
    return spread_rows(jax.random.fold_in(key, 12), SEQUENCE_LENGTH, KDIM)


def draw_value_proj(key, part):
    return spread_rows(jax.random.fold_in(key, 13), SEQUENCE_LENGTH, VDIM)


def head_kinds(key):
    share = 5
    return jax.random.randint(jax.random.fold_in(key, 21), (VALUE_HEADS,), 0, 10) < share


def draw_write_strength(key, part):
    slow_heads = head_kinds(key)
    slow_level = 0.5 * DK / SEQUENCE_LENGTH * jax.random.uniform(jax.random.fold_in(key, 22), (SEQUENCE_LENGTH, VALUE_HEADS), jnp.float32, 0.5, 1.5)
    fast_level = jax.random.uniform(jax.random.fold_in(key, 23), (SEQUENCE_LENGTH, VALUE_HEADS), jnp.float32, 0.1, 0.9)
    return jnp.where(slow_heads[None, :], slow_level, fast_level).astype(jnp.float32)


def draw_log_decay(key, part):
    slow_heads = head_kinds(key)
    slow_rate = jnp.exp(jax.random.uniform(jax.random.fold_in(key, 24), (VALUE_HEADS,), jnp.float32, math.log(0.2), 0.0)) / SEQUENCE_LENGTH
    fast_rate = jnp.exp(jax.random.uniform(jax.random.fold_in(key, 25), (VALUE_HEADS,), jnp.float32, math.log(1.0 / 50.0), math.log(1.0 / 30.0)))
    head_decay_rate = jnp.where(slow_heads, slow_rate, fast_rate)
    approximate_result = jax.random.uniform(jax.random.fold_in(key, 26), (SEQUENCE_LENGTH, VALUE_HEADS), jnp.float32, 0.5, 1.5)
    block_level = jnp.exp(jax.random.uniform(jax.random.fold_in(key, 27), (SEQUENCE_LENGTH // SPAN, VALUE_HEADS), jnp.float32, -0.7, 0.7))
    block_decay_factor = jnp.repeat(block_level, SPAN, axis=0)
    spike_positions = jax.random.randint(jax.random.fold_in(key, 28), (2, VALUE_HEADS), 0, SEQUENCE_LENGTH)
    match_count = jnp.sum((jnp.arange(SEQUENCE_LENGTH)[:, None, None] == spike_positions[None, :, :]).astype(jnp.float32), axis=1)
    spike_penalty = jax.random.uniform(jax.random.fold_in(key, 29), (SEQUENCE_LENGTH, VALUE_HEADS), jnp.float32, 0.2, 0.5)
    spike_component = match_count * jnp.log(1.0 - spike_penalty)
    return (-head_decay_rate[None, :] * approximate_result * block_decay_factor + spike_component).astype(jnp.float32)


def steps_of(rng, dims, cuts, low, top_value):
    level = 1.0
    for axis_at, shards_of in cuts:
        steps = jax.random.uniform(jax.random.fold_in(jax.random.fold_in(rng, 6), axis_at), (shards_of,), jnp.float32, low / len(cuts), top_value / len(cuts))
        level = level * jnp.repeat(jnp.exp(steps), dims[axis_at] // shards_of).reshape((-1,) + (1,) * (len(dims) - 1 - axis_at))
    return level


def normal_values(rng, shape, spread, bound, split=(), held_as=jnp.bfloat16):
    drawn = jax.random.normal(rng, shape, jnp.float32) * spread
    if len(split) > 0:
        drawn = steps_of(rng, shape, split, -0.22, 0.18) * drawn
    return jnp.clip(drawn, min=-bound, max=bound).astype(held_as)


def setup_inputs(seed: int = 0, part: int = 0) -> dict:
    key_list = jax.random.split(jax.random.key(seed), 11)
    own_keys = jax.random.split(jax.random.fold_in(key_list[10], part), 11)
    return {
        "query_proj": draw_query_proj(jax.random.fold_in(jax.random.fold_in(key_list[10], part), 71), part),
        "key_proj": draw_key_proj(jax.random.fold_in(jax.random.fold_in(key_list[10], part), 71), part),
        "value_proj": draw_value_proj(jax.random.fold_in(jax.random.fold_in(key_list[10], part), 71), part),
        "gate_proj": normal_values(own_keys[3], (SEQUENCE_LENGTH, VDIM), 1.0, 6.0, ((0, 8), (1, 2))),
        "write_strength": draw_write_strength(jax.random.fold_in(jax.random.fold_in(key_list[10], part), 71), part),
        "log_decay": draw_log_decay(jax.random.fold_in(jax.random.fold_in(key_list[10], part), 71), part),
        "conv_query": normal_values(key_list[6], (CONV, KDIM), CONV ** -0.5, 3.0, ((1, 2),)),
        "conv_key": normal_values(key_list[7], (CONV, KDIM), CONV ** -0.5, 3.0, ((1, 2),)),
        "conv_value": normal_values(key_list[8], (CONV, VDIM), CONV ** -0.5, 3.0, ((1, 2),)),
        "norm_gain": jnp.clip(1.0 + 0.1 * jax.random.normal(key_list[9], (DV,), jnp.float32), 0.5, 1.5),
    }


precise_setting = lax.Precision.HIGHEST

def conv_silu(rim_rows, source, weights):
    conv_width = weights.shape[0]
    row_count = source.shape[0]
    extended = jnp.concatenate([rim_rows, source], axis=0).astype(jnp.float32)
    weights_f = weights.astype(jnp.float32)
    conv_total = weights_f[0] * extended[0:row_count]
    for offset in range(1, conv_width):
        conv_total = conv_total + weights_f[offset] * extended[offset:offset + row_count]
    return jax.nn.silu(conv_total).astype(jnp.bfloat16)

def unit_heads(matrix, scale_factor):
    row_count = matrix.shape[0]
    heads_split = matrix.astype(jnp.float32).reshape(row_count, matrix.shape[1] // DK, DK)
    squares = lax.optimization_barrier(jnp.sum(heads_split * heads_split, axis=-1, keepdims=True))
    return heads_split * lax.rsqrt(squares + 1e-06) * scale_factor

def blocked(tensor_in):
    block_count = tensor_in.shape[0] // SPAN
    shaped = tensor_in.reshape((block_count, SPAN) + tensor_in.shape[1:])
    order_axes = (2, 0, 1) + tuple(range(3, shaped.ndim))
    return jnp.transpose(shaped, order_axes)

def unit_lower_solve(lower_part, right_side):
    identity_block = jnp.eye(SPAN, dtype=jnp.float32)
    inverse_block = identity_block - lower_part
    power_block = lower_part
    reach = 2
    while reach < SPAN:
        power_block = jnp.einsum('hnij,hnjk->hnik', power_block, power_block, precision=precise_setting)
        inverse_block = jnp.einsum('hnij,hnjk->hnik', inverse_block, identity_block + power_block, precision=precise_setting)
        reach = reach * 2
    return jnp.einsum('hnij,hnjk->hnik', inverse_block, right_side, precision=precise_setting)

def block_terms(query_heads, key_heads, value_conv, strength, log_decay):
    head_count = key_heads.shape[1]
    value_heads = value_conv.astype(jnp.float32).reshape(value_conv.shape[0], head_count, -1)
    query_b = blocked(query_heads)
    key_b = blocked(key_heads)
    value_b = blocked(value_heads)
    strength_b = blocked(strength)
    cumulative = jnp.cumsum(blocked(log_decay), axis=-1)
    positions = jnp.arange(SPAN)
    strictly_below = positions[:, None] > positions[None, :]
    on_or_below = positions[:, None] >= positions[None, :]
    score_gap = cumulative[..., :, None] - cumulative[..., None, :]
    fade_strict = jnp.where(strictly_below, jnp.exp(jnp.where(strictly_below, score_gap, 0.0)), 0.0)
    fade_upto = jnp.where(on_or_below, jnp.exp(jnp.where(on_or_below, score_gap, 0.0)), 0.0)
    key_gram = jnp.einsum('hnik,hnjk->hnij', key_b, key_b, precision=precise_setting)
    lower_part = strength_b[..., :, None] * key_gram * fade_strict
    right_side = jnp.concatenate([strength_b[..., None] * value_b, (strength_b * jnp.exp(cumulative))[..., None] * key_b], axis=-1)
    solved = unit_lower_solve(lower_part, right_side)
    value_width = value_b.shape[-1]
    pseudo_inverse = solved[..., :value_width]
    key_weight_matrix = solved[..., value_width:]
    attention_scores = jnp.einsum('hnik,hnjk->hnij', query_b, key_b, precision=precise_setting) * fade_upto
    final_cumulative = cumulative[..., -1]
    query_decayed = query_b * jnp.exp(cumulative)[..., None]
    key_decayed = key_b * jnp.exp(final_cumulative[..., None] - cumulative)[..., None]
    return (query_decayed, attention_scores, pseudo_inverse, key_weight_matrix, key_decayed, final_cumulative)

def by_block(terms):
    return tuple((jnp.moveaxis(member, 1, 0) for member in terms))

def advance(carried_state, inputs):
    query_decayed, attention_scores, pseudo_inverse, key_weight_matrix, key_decayed, final_cumulative = inputs
    updated_values = pseudo_inverse - jnp.einsum('uqz,uzl->uql', key_weight_matrix, carried_state, precision=precise_setting)
    head_group_block = jnp.einsum('uqz,uzl->uql', query_decayed, carried_state, precision=precise_setting) + jnp.einsum('def,dfk->dek', attention_scores, updated_values, precision=precise_setting)
    carried_state = jnp.exp(final_cumulative)[:, None, None] * carried_state + jnp.einsum('ixe,ixu->ieu', key_decayed, updated_values, precision=precise_setting)
    return (carried_state, head_group_block)

def finish(head_blocks, gate_proj, norm_gain):
    block_count, head_count, span_len, head_width = head_blocks.shape
    row_count = block_count * span_len
    head_rows = jnp.transpose(head_blocks, (0, 2, 1, 3)).reshape(row_count, head_count, head_width)
    mean_square = lax.optimization_barrier(jnp.mean(head_rows * head_rows, axis=-1, keepdims=True))
    gate_rows = gate_proj.astype(jnp.float32).reshape(row_count, head_count, head_width)
    scaled = head_rows * lax.rsqrt(mean_square + 1e-06) * norm_gain.astype(jnp.float32) * jax.nn.silu(gate_rows)
    return scaled.astype(jnp.bfloat16).reshape(row_count, head_count * head_width)

def reference(query_proj, key_proj, value_proj, gate_proj, write_strength, log_decay, conv_query, conv_key, conv_value, norm_gain):
    margin = CONV - 1
    query_conv = conv_silu(jnp.zeros((margin, query_proj.shape[1]), jnp.bfloat16), query_proj, conv_query)
    key_conv = conv_silu(jnp.zeros((margin, key_proj.shape[1]), jnp.bfloat16), key_proj, conv_key)
    value_conv = conv_silu(jnp.zeros((margin, value_proj.shape[1]), jnp.bfloat16), value_proj, conv_value)
    head_ratio = VALUE_HEADS // KH
    query_heads = jnp.repeat(unit_heads(query_conv, DK ** (-0.5)), head_ratio, axis=1)
    key_heads = jnp.repeat(unit_heads(key_conv, 1.0), head_ratio, axis=1)
    terms = block_terms(query_heads, key_heads, value_conv, write_strength, log_decay)
    value_width = value_conv.shape[1] // VALUE_HEADS
    start_state = jnp.zeros((VALUE_HEADS, DK, value_width), jnp.float32)
    final_state, head_blocks = lax.scan(advance, start_state, by_block(terms))
    return finish(head_blocks, gate_proj, norm_gain)
```

```python
import functools

import jax
import jax.numpy as jnp
from jax import lax
from jax.experimental import pallas as pl
from jax.experimental.pallas import tpu as pltpu
from jax.sharding import PartitionSpec as P

DK = 128
RIM = 8
SOLVE_PASSES = 1
F32 = jnp.float32
BF16 = jnp.bfloat16
NN = (((1,), (0,)), ((), ()))
NT = (((1,), (1,)), ((), ()))
TN = (((0,), (0,)), ((), ()))


def pieces(x):
    high = x.astype(BF16)
    return high, (x - high.astype(F32)).astype(BF16)


def dot(a, b, dims=NN):
    return lax.dot_general(a, b, dims, preferred_element_type=F32)


def dot3(a, b, dims=NN):
    ah, al = pieces(a)
    bh, bl = pieces(b)
    return dot(ah, bh, dims) + dot(ah, bl, dims) + dot(al, bh, dims)


def dot1(a, b, dims=NN):
    return dot(a.astype(BF16), b.astype(BF16), dims)


def silu(u):
    return u / (1.0 + jnp.exp(-u))


def conv_silu(rows, rim_ref, source_ref, taps_ref):
    margin = rim_ref.shape[0]
    count = source_ref.shape[0]
    rows[RIM - margin : RIM, :] = rim_ref[...].astype(F32)
    rows[RIM : RIM + count, :] = source_ref[...].astype(F32)
    taps = taps_ref[...].astype(F32)
    total = taps[0:1] * rows[RIM - margin : RIM - margin + count, :]
    for j in range(1, taps.shape[0]):
        total = total + taps[j : j + 1] * rows[RIM - margin + j : RIM - margin + j + count, :]
    return silu(total).astype(BF16).astype(F32)


def unit(x):
    return x * lax.rsqrt(jnp.sum(x * x, axis=-1, keepdims=True) + 1e-06)


def local_kernel(
    ratio,
    rim_q, rim_k, rim_v, q_ref, k_ref, v_ref, beta_ref, decay_ref, tq, tk, tv,
    map_high, map_low, base_ref,
    rows_q, rows_k, rows_v, cum_ref, cum_t_ref,
):
    step = pl.program_id(0)
    count = q_ref.shape[0]
    row = lax.broadcasted_iota(jnp.int32, (count, count), 0)
    column = lax.broadcasted_iota(jnp.int32, (count, count), 1)
    upto = row >= column
    apart = jnp.where(upto, row ^ column, 0)

    @pl.when(step == 0)
    def _():
        ones = upto.astype(F32)
        cum_ref[...] = lax.dot_general(
            ones, decay_ref[...], NN, precision=lax.Precision.HIGHEST, preferred_element_type=F32
        )
        cum_t_ref[...] = lax.dot_general(
            decay_ref[...], ones, (((0,), (1,)), ((), ())),
            precision=lax.Precision.HIGHEST, preferred_element_type=F32,
        )

    query = unit(conv_silu(rows_q, rim_q, q_ref, tq)) * (DK ** -0.5)
    key = unit(conv_silu(rows_k, rim_k, k_ref, tk))
    value = conv_silu(rows_v, rim_v, v_ref, tv)
    gram = dot3(key, key, NT)
    scores = dot3(query, key, NT)
    heads = range(ratio)
    lane = lax.broadcasted_iota(jnp.int32, beta_ref.shape, 1)
    cum, beta, fade, lower = [], [], [], []
    for r in heads:
        head = step * ratio + r
        chosen = lane == head
        c = jnp.sum(jnp.where(chosen, cum_ref[...], 0.0), axis=1, keepdims=True)
        b = jnp.sum(jnp.where(chosen, beta_ref[...], 0.0), axis=1, keepdims=True)
        gap = c - cum_t_ref[pl.ds(head, 1), :]
        f = jnp.where(upto, jnp.exp(jnp.where(upto, gap, 0.0)), 0.0)
        cum.append(c)
        beta.append(b)
        fade.append(f)
        lower.append(b * gram * f)
    identity = (row == column).astype(F32)
    first = apart == 1
    inverse = [identity - jnp.where(first, lower[r], 0.0) for r in heads]
    multiply = dot1 if SOLVE_PASSES == 1 else dot3
    width = 2
    while width < count:
        mask = (apart >= width) & (apart < 2 * width)
        inner = [multiply(jnp.where(mask, lower[r], 0.0), inverse[r]) for r in heads]
        inverse = [inverse[r] - multiply(inverse[r], inner[r]) for r in heads]
        width *= 2
    small = identity[:DK, :DK]
    for r in heads:
        grown = jnp.exp(cum[r])
        right = jnp.concatenate(
            [beta[r] * value[:, r * DK : (r + 1) * DK], (beta[r] * grown) * key], axis=1
        )
        solved = dot3(inverse[r], right)
        last = cum[r][count - 1 : count, :]
        ahead = dot3(key * jnp.exp(last - cum[r]), solved, TN)
        out = dot3(scores * fade[r], solved)
        base_ref[r, 0:DK, :] = ahead[:, :DK]
        base_ref[r, DK : DK + count, :] = out[:, :DK]
        mh, ml = pieces(jnp.exp(last) * small - ahead[:, DK:])
        map_high[r, 0:DK, :] = mh
        map_low[r, 0:DK, :] = ml
        qh, ql = pieces(grown * query - out[:, DK:])
        map_high[r, DK : DK + count, :] = qh
        map_low[r, DK : DK + count, :] = ql


def local_part(rim, query_proj, key_proj, value_proj, beta, decay, conv_q, conv_k, conv_v):
    count = query_proj.shape[0]
    key_heads = query_proj.shape[1] // DK
    heads = beta.shape[1]
    ratio = heads // key_heads
    margin = rim.shape[0]
    width = conv_q.shape[0]
    vw = ratio * DK
    v_first = 2 * key_heads // ratio

    def col(height, w, first=0):
        return pl.BlockSpec((height, w), lambda i: (0, first + i))

    whole = pl.BlockSpec((count, heads), lambda i: (0, 0))
    tall = DK + count
    spec = pl.BlockSpec((ratio, tall, DK), lambda i: (i, 0, 0))
    shape = (heads, tall, DK)
    return pl.pallas_call(
        functools.partial(local_kernel, ratio),
        grid=(key_heads,),
        in_specs=[
            col(margin, DK), col(margin, DK, key_heads), col(margin, vw, v_first),
            col(count, DK), col(count, DK), col(count, vw), whole, whole,
            col(width, DK), col(width, DK), col(width, vw),
        ],
        out_specs=[spec, spec, spec],
        out_shape=[
            jax.ShapeDtypeStruct(shape, BF16),
            jax.ShapeDtypeStruct(shape, BF16),
            jax.ShapeDtypeStruct(shape, F32),
        ],
        scratch_shapes=[
            pltpu.VMEM((RIM + count, DK), F32),
            pltpu.VMEM((RIM + count, DK), F32),
            pltpu.VMEM((RIM + count, vw), F32),
            pltpu.VMEM((count, heads), F32),
            pltpu.VMEM((heads, count), F32),
        ],
        compiler_params=pltpu.CompilerParams(vmem_limit_bytes=40 * 2**20),
        name="local_blocks",
    )(rim, rim, rim, query_proj, key_proj, value_proj, beta, decay, conv_q, conv_k, conv_v)


def relay_kernel(
    n, map_high, map_low, base_ref, gate_ref, gain_ref, out_ref, entering, leaving, send_sem, recv_sem
):
    me = lax.axis_index("seq")
    heads = map_high.shape[0]
    has_left = me > 0
    has_right = me < n - 1
    left = lax.rem(me + n - 1, n)
    right = lax.rem(me + 1, n)
    barrier = pltpu.get_barrier_semaphore()

    @pl.when(has_left)
    def _():
        pl.semaphore_signal(
            barrier, inc=1, device_id={"seq": left}, device_id_type=pl.DeviceIdType.MESH
        )

    @pl.when(has_right)
    def _():
        pl.semaphore_wait(barrier, 1)

    def hop(h):
        return pltpu.make_async_remote_copy(
            src_ref=leaving.at[h],
            dst_ref=entering.at[h],
            send_sem=send_sem.at[h],
            recv_sem=recv_sem.at[h],
            device_id={"seq": right},
            device_id_type=pl.DeviceIdType.MESH,
        )

    @pl.when(jnp.logical_not(has_left))
    def _():
        entering[...] = jnp.zeros_like(entering)

    gain = gain_ref[...]
    for h in range(heads):
        @pl.when(has_left)
        def _():
            hop(h).wait_recv()

        state = entering[h]

        @pl.when(has_right)
        def _():
            ahead = dot(map_high[h, :DK], state) + dot(map_low[h, :DK], state) + base_ref[h, :DK]
            leaving[h] = ahead.astype(leaving.dtype)
            hop(h).start()

        rows = dot(map_high[h, DK:], state) + dot(map_low[h, DK:], state) + base_ref[h, DK:]
        mean = jnp.mean(rows * rows, axis=-1, keepdims=True)
        gate = gate_ref[:, h * DK : (h + 1) * DK].astype(F32)
        out = rows * lax.rsqrt(mean + 1e-06) * gain * silu(gate)
        out_ref[:, h * DK : (h + 1) * DK] = out.astype(BF16)

    @pl.when(has_right)
    def _():
        for h in range(heads):
            hop(h).wait_send()


def relay_part(n, map_high, map_low, base, gate, gain):
    heads = map_high.shape[0]
    vmem = pl.BlockSpec(memory_space=pltpu.VMEM)
    return pl.pallas_call(
        functools.partial(relay_kernel, n),
        in_specs=[vmem] * 5,
        out_specs=vmem,
        out_shape=jax.ShapeDtypeStruct(gate.shape, BF16),
        scratch_shapes=[
            pltpu.VMEM((heads, DK, DK), BF16),
            pltpu.VMEM((heads, DK, DK), BF16),
            pltpu.SemaphoreType.DMA((heads,)),
            pltpu.SemaphoreType.DMA((heads,)),
        ],
        compiler_params=pltpu.CompilerParams(
            collective_id=0, has_side_effects=True, vmem_limit_bytes=40 * 2**20
        ),
        name="relay",
    )(map_high, map_low, base, gate, gain.reshape(1, -1))


def shards(
    query_proj, key_proj, value_proj, gate_proj, write_strength, log_decay,
    conv_query, conv_key, conv_value, norm_gain,
):
    n = lax.axis_size("seq")
    margin = conv_query.shape[0] - 1
    tails = jnp.concatenate(
        [query_proj[-margin:], key_proj[-margin:], value_proj[-margin:]], axis=1
    )
    rim = lax.ppermute(tails, "seq", [(i, i + 1) for i in range(n - 1)])
    parts = local_part(
        rim, query_proj, key_proj, value_proj, write_strength, log_decay,
        conv_query, conv_key, conv_value,
    )
    return relay_part(n, *parts, gate_proj, norm_gain)


def solution(mesh):
    split = P(("groups", "seq"), "head")
    in_specs = (split,) * 6 + (P(None, "head"),) * 3 + (P(),)
    return jax.shard_map(shards, mesh=mesh, in_specs=in_specs, out_specs=split, check_vma=False)
```

```python
import functools

import jax
import jax.numpy as jnp
from jax import lax
from jax.experimental import pallas as pl
from jax.experimental.pallas import tpu as pltpu
from jax.sharding import PartitionSpec as P

DK = 128
TILE = 16
KEY_HEADS_A_STEP = 2
F32 = jnp.float32
BF16 = jnp.bfloat16
NN = (((1,), (0,)), ((), ()))
NT = (((1,), (1,)), ((), ()))
TN = (((0,), (0,)), ((), ()))


def pieces(x):
    high = x.astype(BF16)
    return high, (x - high.astype(F32)).astype(BF16)


def dot(a, b, dims=NN):
    return lax.dot_general(a, b, dims, preferred_element_type=F32)


def dot3(a, b, dims=NN):
    ah, al = pieces(a)
    bh, bl = pieces(b)
    return dot(ah, bh, dims) + dot(ah, bl, dims) + dot(al, bh, dims)


def dot1(a, b, dims=NN):
    return dot(a.astype(BF16), b.astype(BF16), dims)


def silu(u):
    return u / (1.0 + jnp.exp(-u))


def dot2(a, b, dims=NN):
    bh, bl = pieces(b)
    a = a.astype(BF16)
    return dot(a, bh, dims) + dot(a, bl, dims)


def precise(a, b, dims):
    return lax.dot_general(
        a, b, dims, precision=lax.Precision.HIGHEST, preferred_element_type=F32
    )


def conv_silu(rows, rim, source_ref, taps_ref):
    count = source_ref.shape[0]
    rows[0:TILE, :] = rim.astype(F32)
    rows[TILE : TILE + count, :] = source_ref[...].astype(F32)
    taps = taps_ref[...].astype(F32)
    first = TILE - taps.shape[0] + 1
    total = taps[0:1] * rows[first : first + count, :]
    for j in range(1, taps.shape[0]):
        total = total + taps[j : j + 1] * rows[first + j : first + j + count, :]
    return silu(total).astype(BF16).astype(F32)


def unit(x):
    return x * lax.rsqrt(jnp.sum(x * x, axis=-1, keepdims=True) + 1e-06)


def kernel(
    n, ratio, per_step, steps,
    tail_q, tail_k, tail_v, q_ref, k_ref, v_ref, beta_t, decay_t, tq, tk, tv, gate_ref, gain_ref,
    out_ref,
    rows_q, rows_k, rows_v, cum_ref, cum_t_ref, beta_ref,
    map_high, map_low, reader, base_ref, rim_q, rim_k, rim_v, entering, leaving,
    send_sem, recv_sem, rim_send, rim_recv,
):
    step = pl.program_id(0)
    me = lax.axis_index("seq")
    has_left = me > 0
    has_right = me < n - 1
    left = lax.rem(me + n - 1, n)
    right = lax.rem(me + 1, n)
    count = q_ref.shape[0]
    group = ratio * per_step
    total_heads = group * steps
    row = lax.broadcasted_iota(jnp.int32, (count, count), 0)
    column = lax.broadcasted_iota(jnp.int32, (count, count), 1)
    upto = row >= column
    apart = jnp.where(upto, row ^ column, 0)
    identity = (row == column).astype(F32)

    def rim_hop(i):
        source, target = ((tail_q, rim_q), (tail_k, rim_k), (tail_v, rim_v))[i]
        return pltpu.make_async_remote_copy(
            src_ref=source, dst_ref=target, send_sem=rim_send.at[i], recv_sem=rim_recv.at[i],
            device_id={"seq": right}, device_id_type=pl.DeviceIdType.MESH,
        )

    def hop(h):
        return pltpu.make_async_remote_copy(
            src_ref=leaving.at[h], dst_ref=entering.at[h],
            send_sem=send_sem.at[h], recv_sem=recv_sem.at[h],
            device_id={"seq": right}, device_id_type=pl.DeviceIdType.MESH,
        )

    @pl.when(step == 0)
    def _():
        barrier = pltpu.get_barrier_semaphore()

        @pl.when(has_left)
        def _():
            pl.semaphore_signal(
                barrier, inc=1, device_id={"seq": left}, device_id_type=pl.DeviceIdType.MESH
            )

        @pl.when(has_right)
        def _():
            pl.semaphore_wait(barrier, 1)
            for i in range(3):
                rim_hop(i).start()

        ones = upto.astype(F32)
        cum_ref[...] = precise(ones, decay_t[...], NT)
        cum_t_ref[...] = precise(decay_t[...], ones, NT)
        beta_ref[...] = precise(identity, beta_t[...], NT)

        @pl.when(jnp.logical_not(has_left))
        def _():
            entering[...] = jnp.zeros_like(entering)
            for ref in (rim_q, rim_k, rim_v):
                ref[...] = jnp.zeros_like(ref)

        @pl.when(has_left)
        def _():
            for i in range(3):
                rim_hop(i).wait_recv()

        @pl.when(has_right)
        def _():
            for i in range(3):
                rim_hop(i).wait_send()

    def rim_of(ref, w):
        return ref[:, pl.ds(pl.multiple_of(step * w, 128), w)]

    kw = per_step * DK
    vw = group * DK
    query_all = conv_silu(rows_q, rim_of(rim_q, kw), q_ref, tq)
    key_all = conv_silu(rows_k, rim_of(rim_k, kw), k_ref, tk)
    value = conv_silu(rows_v, rim_of(rim_v, vw), v_ref, tv)
    queries = [unit(query_all[:, g * DK : (g + 1) * DK]) * (DK ** -0.5) for g in range(per_step)]
    keys = [unit(key_all[:, g * DK : (g + 1) * DK]) for g in range(per_step)]
    grams = [dot3(keys[g], keys[g], NT) for g in range(per_step)]
    scores = [dot3(queries[g], keys[g], NT) for g in range(per_step)]
    heads = range(group)
    lane = lax.broadcasted_iota(jnp.int32, beta_ref.shape, 1)
    cum, beta, fade, lower = [], [], [], []
    for r in heads:
        head = step * group + r
        chosen = lane == head
        c = jnp.sum(jnp.where(chosen, cum_ref[...], 0.0), axis=1, keepdims=True)
        b = jnp.sum(jnp.where(chosen, beta_ref[...], 0.0), axis=1, keepdims=True)
        gap = c - cum_t_ref[pl.ds(head, 1), :]
        f = jnp.where(upto, jnp.exp(jnp.where(upto, gap, 0.0)), 0.0)
        cum.append(c)
        beta.append(b)
        fade.append(f)
        lower.append(b * grams[r // ratio] * f)
    inverse = [identity - jnp.where(apart == 1, lower[r], 0.0) for r in heads]
    width = 2
    while width < count:
        mask = (apart >= width) & (apart < 2 * width)
        low = [inverse[r].astype(BF16) for r in heads]
        inner = [dot(jnp.where(mask, lower[r], 0.0).astype(BF16), low[r]) for r in heads]
        inverse = [inverse[r] - dot(low[r], inner[r].astype(BF16)) for r in heads]
        width *= 2
    small = identity[:DK, :DK]
    grown = [jnp.exp(cum[r]) for r in heads]
    solved = []
    for r in heads:
        rhs = jnp.concatenate(
            [
                beta[r] * value[:, r * DK : (r + 1) * DK],
                (beta[r] * grown[r]) * keys[r // ratio],
            ],
            axis=1,
        )
        solved.append(dot3(inverse[r], rhs))
    for r in heads:
        head = step * group + r
        last = cum[r][count - 1 : count, :]
        faded = keys[r // ratio] * jnp.exp(last - cum[r])
        ahead = dot2(faded, solved[r], TN)
        out = dot1(scores[r // ratio] * fade[r], solved[r])
        base_ref[head, 0:DK, :] = ahead[:, :DK]
        base_ref[head, DK : DK + count, :] = out[:, :DK]
        mh, ml = pieces(jnp.exp(last) * small - ahead[:, DK:])
        map_high[head] = mh
        map_low[head] = ml
        reader[head] = (grown[r] * queries[r // ratio] - out[:, DK:]).astype(BF16)

    def step_state(h):
        state = entering[h]
        new = dot(map_high[h], state) + dot(map_low[h], state) + base_ref[h, 0:DK, :]
        leaving[h] = new.astype(BF16)

    def forward(p):
        @pl.when(has_left)
        def _():
            for r in heads:
                hop(p * group + r).wait_recv()

        @pl.when(has_right)
        def _():
            for r in heads:
                step_state(p * group + r)
            for r in heads:
                hop(p * group + r).start()

    def forward_each(p):
        for r in heads:
            h = p * group + r

            @pl.when(has_left)
            def _():
                hop(h).wait_recv()

            @pl.when(has_right)
            def _():
                step_state(h)
                hop(h).start()

    gain = gain_ref[...]

    def finish(p):
        for r in heads:
            h = p * group + r
            place = pl.ds(pl.multiple_of(h * DK, DK), DK)
            rows = dot(reader[h], entering[h]) + base_ref[h, DK : DK + count, :]
            mean = jnp.mean(rows * rows, axis=-1, keepdims=True)
            gate = gate_ref[:, place].astype(F32)
            out_ref[:, place] = (rows * lax.rsqrt(mean + 1e-06) * gain * silu(gate)).astype(BF16)

    @pl.when(step >= me)
    def _():
        forward(step - me)

    @pl.when(step == steps - 1)
    def _():
        start = jnp.maximum(steps - me, 0)

        @pl.loop(start, steps)
        def _(p):
            forward_each(p)
            finish(p)

        @pl.loop(0, start)
        def _(p):
            finish(p)

        @pl.when(has_right)
        def _():
            for h in range(total_heads):
                hop(h).wait_send()


def shards(
    query_proj, key_proj, value_proj, gate_proj, write_strength, log_decay,
    conv_query, conv_key, conv_value, norm_gain,
):
    n = lax.axis_size("seq")
    count = query_proj.shape[0]
    key_heads = query_proj.shape[1] // DK
    heads = write_strength.shape[1]
    ratio = heads // key_heads
    per_step = KEY_HEADS_A_STEP
    steps = key_heads // per_step
    taps = conv_query.shape[0]
    kw = per_step * DK
    vw = ratio * kw

    def col(height, w):
        return pl.BlockSpec((height, w), lambda i: (0, i))

    def whole(x):
        return pl.BlockSpec(x.shape, lambda i: (0, 0))

    def tail(x):
        return pl.BlockSpec((TILE, x.shape[1]), lambda i: (count // TILE - 1, 0))

    beta_t = write_strength.T
    decay_t = log_decay.T
    gain = norm_gain.reshape(1, -1)
    return pl.pallas_call(
        functools.partial(kernel, n, ratio, per_step, steps),
        grid=(steps,),
        in_specs=[
            tail(query_proj), tail(key_proj), tail(value_proj),
            col(count, kw), col(count, kw), col(count, vw), whole(beta_t), whole(decay_t),
            col(taps, kw), col(taps, kw), col(taps, vw), whole(gate_proj), whole(gain),
        ],
        out_specs=whole(gate_proj),
        out_shape=jax.ShapeDtypeStruct(gate_proj.shape, BF16),
        scratch_shapes=[
            pltpu.VMEM((TILE + count, kw), F32),
            pltpu.VMEM((TILE + count, kw), F32),
            pltpu.VMEM((TILE + count, vw), F32),
            pltpu.VMEM((count, heads), F32),
            pltpu.VMEM((heads, count), F32),
            pltpu.VMEM((count, heads), F32),
            pltpu.VMEM((heads, DK, DK), BF16),
            pltpu.VMEM((heads, DK, DK), BF16),
            pltpu.VMEM((heads, count, DK), BF16),
            pltpu.VMEM((heads, DK + count, DK), F32),
            pltpu.VMEM((TILE, query_proj.shape[1]), BF16),
            pltpu.VMEM((TILE, key_proj.shape[1]), BF16),
            pltpu.VMEM((TILE, value_proj.shape[1]), BF16),
            pltpu.VMEM((heads, DK, DK), BF16),
            pltpu.VMEM((heads, DK, DK), BF16),
            pltpu.SemaphoreType.DMA((heads,)),
            pltpu.SemaphoreType.DMA((heads,)),
            pltpu.SemaphoreType.DMA((3,)),
            pltpu.SemaphoreType.DMA((3,)),
        ],
        compiler_params=pltpu.CompilerParams(
            collective_id=0, has_side_effects=True, vmem_limit_bytes=56 * 2**20
        ),
        name="delta_layer",
    )(
        query_proj, key_proj, value_proj, query_proj, key_proj, value_proj, beta_t, decay_t,
        conv_query, conv_key, conv_value, gate_proj, gain,
    )


def solution(mesh):
    split = P(("groups", "seq"), "head")
    in_specs = (split,) * 6 + (P(None, "head"),) * 3 + (P(),)
    return jax.shard_map(shards, mesh=mesh, in_specs=in_specs, out_specs=split, check_vma=False)
```

```python
import functools

import jax
import jax.numpy as jnp
from jax import lax
from jax.experimental import pallas as pl
from jax.experimental.pallas import tpu as pltpu
from jax.sharding import PartitionSpec as P

DK = 128
TILE = 16
KEY_HEADS_A_STEP = 2
BLOCK = 64
F32 = jnp.float32
BF16 = jnp.bfloat16
NN = (((1,), (0,)), ((), ()))
NT = (((1,), (1,)), ((), ()))
TN = (((0,), (0,)), ((), ()))


def pieces(x):
    high = x.astype(BF16)
    return high, (x - high.astype(F32)).astype(BF16)


def dot(a, b, dims=NN):
    return lax.dot_general(a, b, dims, preferred_element_type=F32)


def dot3(a, b, dims=NN):
    ah, al = pieces(a)
    bh, bl = pieces(b)
    return dot(ah, bh, dims) + dot(ah, bl, dims) + dot(al, bh, dims)


def dot1(a, b, dims=NN):
    return dot(a.astype(BF16), b.astype(BF16), dims)


def silu(u):
    return u / (1.0 + jnp.exp(-u))


def dot2(a, b, dims=NN):
    bh, bl = pieces(b)
    a = a.astype(BF16)
    return dot(a, bh, dims) + dot(a, bl, dims)


def precise(a, b, dims):
    return lax.dot_general(
        a, b, dims, precision=lax.Precision.HIGHEST, preferred_element_type=F32
    )


def conv_silu(rows, rim, source_ref, taps_ref):
    count = source_ref.shape[0]
    rows[0:TILE, :] = rim.astype(F32)
    rows[TILE : TILE + count, :] = source_ref[...].astype(F32)
    taps = taps_ref[...].astype(F32)
    first = TILE - taps.shape[0] + 1
    total = taps[0:1] * rows[first : first + count, :]
    for j in range(1, taps.shape[0]):
        total = total + taps[j : j + 1] * rows[first + j : first + j + count, :]
    return silu(total).astype(BF16).astype(F32)


def unit(x):
    return x * lax.rsqrt(jnp.sum(x * x, axis=-1, keepdims=True) + 1e-06)


def kernel(
    n, ratio, per_step, steps,
    tail_q, tail_k, tail_v, q_ref, k_ref, v_ref, beta_t, decay_t, tq, tk, tv, gate_ref, gain_ref,
    out_ref,
    rows_q, rows_k, rows_v, cum_ref, cum_t_ref, beta_ref,
    map_high, map_low, reader, base_ref, rim_q, rim_k, rim_v, entering, leaving,
    send_sem, recv_sem, rim_send, rim_recv,
):
    step = pl.program_id(0)
    me = lax.axis_index("seq")
    has_left = me > 0
    has_right = me < n - 1
    left = lax.rem(me + n - 1, n)
    right = lax.rem(me + 1, n)
    count = q_ref.shape[0]
    group = ratio * per_step
    total_heads = group * steps
    row = lax.broadcasted_iota(jnp.int32, (count, count), 0)
    column = lax.broadcasted_iota(jnp.int32, (count, count), 1)
    upto = row >= column
    apart = jnp.where(upto, row ^ column, 0)
    identity = (row == column).astype(F32)

    def rim_hop(i):
        source, target = ((tail_q, rim_q), (tail_k, rim_k), (tail_v, rim_v))[i]
        return pltpu.make_async_remote_copy(
            src_ref=source, dst_ref=target, send_sem=rim_send.at[i], recv_sem=rim_recv.at[i],
            device_id={"seq": right}, device_id_type=pl.DeviceIdType.MESH,
        )

    def hop(h):
        return pltpu.make_async_remote_copy(
            src_ref=leaving.at[h], dst_ref=entering.at[h],
            send_sem=send_sem.at[h], recv_sem=recv_sem.at[h],
            device_id={"seq": right}, device_id_type=pl.DeviceIdType.MESH,
        )

    @pl.when(step == 0)
    def _():
        barrier = pltpu.get_barrier_semaphore()

        @pl.when(has_left)
        def _():
            pl.semaphore_signal(
                barrier, inc=1, device_id={"seq": left}, device_id_type=pl.DeviceIdType.MESH
            )

        @pl.when(has_right)
        def _():
            pl.semaphore_wait(barrier, 1)
            for i in range(3):
                rim_hop(i).start()

        ones = upto.astype(F32)
        cum_ref[...] = precise(ones, decay_t[...], NT)
        cum_t_ref[...] = precise(decay_t[...], ones, NT)
        beta_ref[...] = precise(identity, beta_t[...], NT)

        @pl.when(jnp.logical_not(has_left))
        def _():
            entering[...] = jnp.zeros_like(entering)
            for ref in (rim_q, rim_k, rim_v):
                ref[...] = jnp.zeros_like(ref)

        @pl.when(has_left)
        def _():
            for i in range(3):
                rim_hop(i).wait_recv()

        @pl.when(has_right)
        def _():
            for i in range(3):
                rim_hop(i).wait_send()

    def rim_of(ref, w):
        return ref[:, pl.ds(pl.multiple_of(step * w, 128), w)]

    kw = per_step * DK
    vw = group * DK
    query_all = conv_silu(rows_q, rim_of(rim_q, kw), q_ref, tq)
    key_all = conv_silu(rows_k, rim_of(rim_k, kw), k_ref, tk)
    value = conv_silu(rows_v, rim_of(rim_v, vw), v_ref, tv)
    queries = [unit(query_all[:, g * DK : (g + 1) * DK]) * (DK ** -0.5) for g in range(per_step)]
    keys = [unit(key_all[:, g * DK : (g + 1) * DK]) for g in range(per_step)]
    grams = [dot3(keys[g], keys[g], NT) for g in range(per_step)]
    scores = [dot3(queries[g], keys[g], NT) for g in range(per_step)]
    heads = range(group)
    lane = lax.broadcasted_iota(jnp.int32, beta_ref.shape, 1)
    cum, beta, fade, lower = [], [], [], []
    for r in heads:
        head = step * group + r
        chosen = lane == head
        c = jnp.sum(jnp.where(chosen, cum_ref[...], 0.0), axis=1, keepdims=True)
        b = jnp.sum(jnp.where(chosen, beta_ref[...], 0.0), axis=1, keepdims=True)
        gap = c - cum_t_ref[pl.ds(head, 1), :]
        f = jnp.where(upto, jnp.exp(jnp.where(upto, gap, 0.0)), 0.0)
        cum.append(c)
        beta.append(b)
        fade.append(f)
        lower.append(b * grams[r // ratio] * f)
    blocks = count // BLOCK
    row_p = lax.broadcasted_iota(jnp.int32, (BLOCK, count), 0)
    lane_p = lax.broadcasted_iota(jnp.int32, (BLOCK, count), 1)
    apart_p = jnp.where(row_p >= lane_p % BLOCK, row_p ^ (lane_p % BLOCK), 0)
    eye_p = (row_p == lane_p % BLOCK).astype(F32)
    same_block = row // BLOCK == column // BLOCK
    keep = same_block.astype(F32).astype(BF16)

    def pack(x):
        packed = x[0:BLOCK, :]
        for b in range(1, blocks):
            packed = jnp.where(lane_p // BLOCK == b, x[b * BLOCK : (b + 1) * BLOCK, :], packed)
        return packed

    def spread(x):
        return jnp.concatenate([x] * blocks, axis=0) * keep

    lower_p = [pack(lower[r]) for r in heads]
    inverse = [eye_p - jnp.where(apart_p == 1, lower_p[r], 0.0) for r in heads]
    width = 2
    while width < BLOCK:
        mask = (apart_p >= width) & (apart_p < 2 * width)
        low = [inverse[r].astype(BF16) for r in heads]
        inner = [
            dot(jnp.where(mask, lower_p[r], 0.0).astype(BF16), spread(low[r])) for r in heads
        ]
        inverse = [inverse[r] - dot(low[r], spread(inner[r].astype(BF16))) for r in heads]
        width *= 2
    inverse = [
        jnp.where(same_block, jnp.concatenate([inverse[r]] * blocks, axis=0), 0.0) for r in heads
    ]
    while width < count:
        mask = (apart >= width) & (apart < 2 * width)
        low = [inverse[r].astype(BF16) for r in heads]
        inner = [dot(jnp.where(mask, lower[r], 0.0).astype(BF16), low[r]) for r in heads]
        inverse = [inverse[r] - dot(low[r], inner[r].astype(BF16)) for r in heads]
        width *= 2
    small = identity[:DK, :DK]
    grown = [jnp.exp(cum[r]) for r in heads]
    solved = []
    for r in heads:
        rhs = jnp.concatenate(
            [
                beta[r] * value[:, r * DK : (r + 1) * DK],
                (beta[r] * grown[r]) * keys[r // ratio],
            ],
            axis=1,
        )
        solved.append(dot2(inverse[r], rhs))
    for r in heads:
        head = step * group + r
        last = cum[r][count - 1 : count, :]
        faded = keys[r // ratio] * jnp.exp(last - cum[r])
        ahead = dot2(faded, solved[r], TN)
        out = dot1(scores[r // ratio] * fade[r], solved[r])
        base_ref[head, 0:DK, :] = ahead[:, :DK]
        base_ref[head, DK : DK + count, :] = out[:, :DK]
        mh, ml = pieces(jnp.exp(last) * small - ahead[:, DK:])
        map_high[head] = mh
        map_low[head] = ml
        reader[head] = (grown[r] * queries[r // ratio] - out[:, DK:]).astype(BF16)

    def step_state(h):
        state = entering[h]
        new = dot(map_high[h], state) + dot(map_low[h], state) + base_ref[h, 0:DK, :]
        leaving[h] = new.astype(BF16)

    def forward(p):
        @pl.when(has_left)
        def _():
            for r in heads:
                hop(p * group + r).wait_recv()

        @pl.when(has_right)
        def _():
            for r in heads:
                step_state(p * group + r)
            for r in heads:
                hop(p * group + r).start()

    def forward_each(p):
        for r in heads:
            h = p * group + r

            @pl.when(has_left)
            def _():
                hop(h).wait_recv()

            @pl.when(has_right)
            def _():
                step_state(h)
                hop(h).start()

    gain = gain_ref[...]

    def finish(p):
        for r in heads:
            h = p * group + r
            place = pl.ds(pl.multiple_of(h * DK, DK), DK)
            rows = dot(reader[h], entering[h]) + base_ref[h, DK : DK + count, :]
            mean = jnp.mean(rows * rows, axis=-1, keepdims=True)
            gate = gate_ref[:, place].astype(F32)
            out_ref[:, place] = (rows * lax.rsqrt(mean + 1e-06) * gain * silu(gate)).astype(BF16)

    @pl.when(step >= me)
    def _():
        forward(step - me)

    @pl.when(step == steps - 1)
    def _():
        start = jnp.maximum(steps - me, 0)

        @pl.loop(start, steps)
        def _(p):
            forward_each(p)
            finish(p)

        @pl.loop(0, start)
        def _(p):
            finish(p)

        @pl.when(has_right)
        def _():
            for h in range(total_heads):
                hop(h).wait_send()


def shards(
    query_proj, key_proj, value_proj, gate_proj, write_strength, log_decay,
    conv_query, conv_key, conv_value, norm_gain,
):
    n = lax.axis_size("seq")
    count = query_proj.shape[0]
    key_heads = query_proj.shape[1] // DK
    heads = write_strength.shape[1]
    ratio = heads // key_heads
    per_step = KEY_HEADS_A_STEP
    steps = key_heads // per_step
    taps = conv_query.shape[0]
    kw = per_step * DK
    vw = ratio * kw

    def col(height, w):
        return pl.BlockSpec((height, w), lambda i: (0, i))

    def whole(x):
        return pl.BlockSpec(x.shape, lambda i: (0, 0))

    def tail(x):
        return pl.BlockSpec((TILE, x.shape[1]), lambda i: (count // TILE - 1, 0))

    beta_t = write_strength.T
    decay_t = log_decay.T
    gain = norm_gain.reshape(1, -1)
    return pl.pallas_call(
        functools.partial(kernel, n, ratio, per_step, steps),
        grid=(steps,),
        in_specs=[
            tail(query_proj), tail(key_proj), tail(value_proj),
            col(count, kw), col(count, kw), col(count, vw), whole(beta_t), whole(decay_t),
            col(taps, kw), col(taps, kw), col(taps, vw), whole(gate_proj), whole(gain),
        ],
        out_specs=pl.BlockSpec(memory_space=pltpu.VMEM),
        out_shape=jax.ShapeDtypeStruct(gate_proj.shape, BF16),
        scratch_shapes=[
            pltpu.VMEM((TILE + count, kw), F32),
            pltpu.VMEM((TILE + count, kw), F32),
            pltpu.VMEM((TILE + count, vw), F32),
            pltpu.VMEM((count, heads), F32),
            pltpu.VMEM((heads, count), F32),
            pltpu.VMEM((count, heads), F32),
            pltpu.VMEM((heads, DK, DK), BF16),
            pltpu.VMEM((heads, DK, DK), BF16),
            pltpu.VMEM((heads, count, DK), BF16),
            pltpu.VMEM((heads, DK + count, DK), F32),
            pltpu.VMEM((TILE, query_proj.shape[1]), BF16),
            pltpu.VMEM((TILE, key_proj.shape[1]), BF16),
            pltpu.VMEM((TILE, value_proj.shape[1]), BF16),
            pltpu.VMEM((heads, DK, DK), BF16),
            pltpu.VMEM((heads, DK, DK), BF16),
            pltpu.SemaphoreType.DMA((heads,)),
            pltpu.SemaphoreType.DMA((heads,)),
            pltpu.SemaphoreType.DMA((3,)),
            pltpu.SemaphoreType.DMA((3,)),
        ],
        compiler_params=pltpu.CompilerParams(
            collective_id=0, has_side_effects=True, vmem_limit_bytes=56 * 2**20
        ),
        name="delta_layer",
    )(
        query_proj, key_proj, value_proj, query_proj, key_proj, value_proj, beta_t, decay_t,
        conv_query, conv_key, conv_value, gate_proj, gain,
    )


def solution(mesh):
    split = P(("groups", "seq"), "head")
    in_specs = (split,) * 6 + (P(None, "head"),) * 3 + (P(),)
    return jax.shard_map(shards, mesh=mesh, in_specs=in_specs, out_specs=split, check_vma=False)
```

```python
import functools

import jax
import jax.numpy as jnp
from jax import lax
from jax.experimental import pallas as pl
from jax.experimental.pallas import tpu as pltpu
from jax.sharding import PartitionSpec as P

DK = 128
TILE = 16
KEY_HEADS_A_STEP = 2
BLOCK = 64
F32 = jnp.float32
BF16 = jnp.bfloat16
NN = (((1,), (0,)), ((), ()))
NT = (((1,), (1,)), ((), ()))
TN = (((0,), (0,)), ((), ()))


def pieces(x):
    high = x.astype(BF16)
    return high, (x - high.astype(F32)).astype(BF16)


def dot(a, b, dims=NN):
    return lax.dot_general(a, b, dims, preferred_element_type=F32)


def dot3(a, b, dims=NN):
    ah, al = pieces(a)
    bh, bl = pieces(b)
    return dot(ah, bh, dims) + dot(ah, bl, dims) + dot(al, bh, dims)


def dot1(a, b, dims=NN):
    return dot(a.astype(BF16), b.astype(BF16), dims)


def silu(u):
    return u / (1.0 + jnp.exp(-u))


def dot2(a, b, dims=NN):
    bh, bl = pieces(b)
    a = a.astype(BF16)
    return dot(a, bh, dims) + dot(a, bl, dims)


def precise(a, b, dims):
    return lax.dot_general(
        a, b, dims, precision=lax.Precision.HIGHEST, preferred_element_type=F32
    )


def conv_silu(rows, rim, source_ref, taps_ref):
    count = source_ref.shape[0]
    rows[0:TILE, :] = rim.astype(F32)
    rows[TILE : TILE + count, :] = source_ref[...].astype(F32)
    taps = taps_ref[...].astype(F32)
    first = TILE - taps.shape[0] + 1
    total = taps[0:1] * rows[first : first + count, :]
    for j in range(1, taps.shape[0]):
        total = total + taps[j : j + 1] * rows[first + j : first + j + count, :]
    return silu(total).astype(BF16).astype(F32)


def unit(x):
    return x * lax.rsqrt(jnp.sum(x * x, axis=-1, keepdims=True) + 1e-06)


def kernel(
    n, ratio, per_step, steps,
    tail_q, tail_k, tail_v, q_ref, k_ref, v_ref, beta_t, decay_t, tq, tk, tv, gate_ref, gain_ref,
    out_ref,
    rows_q, rows_k, rows_v, cum_ref, cum_t_ref, beta_ref,
    map_high, map_low, reader, base_ref, rim_q, rim_k, rim_v, entering, leaving,
    send_sem, recv_sem, rim_send, rim_recv,
):
    step = pl.program_id(0)
    me = lax.axis_index("seq")
    has_left = me > 0
    has_right = me < n - 1
    left = lax.rem(me + n - 1, n)
    right = lax.rem(me + 1, n)
    count = q_ref.shape[0]
    group = ratio * per_step
    total_heads = group * steps
    heads = range(group)
    row = lax.broadcasted_iota(jnp.int32, (count, count), 0)
    column = lax.broadcasted_iota(jnp.int32, (count, count), 1)
    upto = row >= column
    apart = jnp.where(upto, row ^ column, 0)
    identity = (row == column).astype(F32)

    def rim_hop(i):
        source, target = ((tail_q, rim_q), (tail_k, rim_k), (tail_v, rim_v))[i]
        return pltpu.make_async_remote_copy(
            src_ref=source, dst_ref=target, send_sem=rim_send.at[i], recv_sem=rim_recv.at[i],
            device_id={"seq": right}, device_id_type=pl.DeviceIdType.MESH,
        )

    def hop(h):
        return pltpu.make_async_remote_copy(
            src_ref=leaving.at[h], dst_ref=entering.at[h],
            send_sem=send_sem.at[h], recv_sem=recv_sem.at[h],
            device_id={"seq": right}, device_id_type=pl.DeviceIdType.MESH,
        )

    @pl.when(step == 0)
    def _():
        barrier = pltpu.get_barrier_semaphore()

        @pl.when(has_left)
        def _():
            pl.semaphore_signal(
                barrier, inc=1, device_id={"seq": left}, device_id_type=pl.DeviceIdType.MESH
            )

        @pl.when(has_right)
        def _():
            pl.semaphore_wait(barrier, 1)
            for i in range(3):
                rim_hop(i).start()

        ones = upto.astype(F32)
        cum_ref[...] = precise(ones, decay_t[...], NT)
        cum_t_ref[...] = precise(decay_t[...], ones, NT)
        beta_ref[...] = precise(identity, beta_t[...], NT)

        @pl.when(jnp.logical_not(has_left))
        def _():
            entering[...] = jnp.zeros_like(entering)
            for ref in (rim_q, rim_k, rim_v):
                ref[...] = jnp.zeros_like(ref)

        @pl.when(has_left)
        def _():
            for i in range(3):
                rim_hop(i).wait_recv()

        @pl.when(has_right)
        def _():
            for i in range(3):
                rim_hop(i).wait_send()

    def rim_of(ref, w):
        return ref[:, pl.ds(pl.multiple_of(step * w, 128), w)]

    def step_state(h):
        state = entering[h]
        new = dot(map_high[h], state) + dot(map_low[h], state) + base_ref[h, 0:DK, :]
        leaving[h] = new.astype(BF16)

    def forward(p):
        @pl.when(has_left)
        def _():
            for r in heads:
                hop(p * group + r).wait_recv()

        @pl.when(has_right)
        def _():
            for r in heads:
                step_state(p * group + r)
            for r in heads:
                hop(p * group + r).start()

    def forward_each(p):
        for r in heads:
            h = p * group + r

            @pl.when(has_left)
            def _():
                hop(h).wait_recv()

            @pl.when(has_right)
            def _():
                step_state(h)
                hop(h).start()

    lag = (me + 1) // 2
    odd = me % 2 == 1
    ready = step >= lag

    kw = per_step * DK
    vw = group * DK
    query_all = conv_silu(rows_q, rim_of(rim_q, kw), q_ref, tq)
    key_all = conv_silu(rows_k, rim_of(rim_k, kw), k_ref, tk)
    value = conv_silu(rows_v, rim_of(rim_v, vw), v_ref, tv)
    queries = [unit(query_all[:, g * DK : (g + 1) * DK]) * (DK ** -0.5) for g in range(per_step)]
    keys = [unit(key_all[:, g * DK : (g + 1) * DK]) for g in range(per_step)]
    grams = [dot3(keys[g], keys[g], NT) for g in range(per_step)]
    scores = [dot3(queries[g], keys[g], NT) for g in range(per_step)]
    lane = lax.broadcasted_iota(jnp.int32, beta_ref.shape, 1)
    cum, beta, fade, lower = [], [], [], []
    for r in heads:
        head = step * group + r
        chosen = lane == head
        c = jnp.sum(jnp.where(chosen, cum_ref[...], 0.0), axis=1, keepdims=True)
        b = jnp.sum(jnp.where(chosen, beta_ref[...], 0.0), axis=1, keepdims=True)
        gap = c - cum_t_ref[pl.ds(head, 1), :]
        f = jnp.where(upto, jnp.exp(jnp.where(upto, gap, 0.0)), 0.0)
        cum.append(c)
        beta.append(b)
        fade.append(f)
        lower.append(b * grams[r // ratio] * f)
    blocks = count // BLOCK
    row_p = lax.broadcasted_iota(jnp.int32, (BLOCK, count), 0)
    lane_p = lax.broadcasted_iota(jnp.int32, (BLOCK, count), 1)
    apart_p = jnp.where(row_p >= lane_p % BLOCK, row_p ^ (lane_p % BLOCK), 0)
    eye_p = (row_p == lane_p % BLOCK).astype(F32)
    same_block = row // BLOCK == column // BLOCK
    keep = same_block.astype(F32).astype(BF16)

    def pack(x):
        packed = x[0:BLOCK, :]
        for b in range(1, blocks):
            packed = jnp.where(lane_p // BLOCK == b, x[b * BLOCK : (b + 1) * BLOCK, :], packed)
        return packed

    def spread(x):
        return jnp.concatenate([x] * blocks, axis=0) * keep

    lower_p = [pack(lower[r]) for r in heads]
    inverse = [eye_p - jnp.where(apart_p == 1, lower_p[r], 0.0) for r in heads]
    width = 2
    while width < BLOCK:
        mask = (apart_p >= width) & (apart_p < 2 * width)
        low = [inverse[r].astype(BF16) for r in heads]
        inner = [
            dot(jnp.where(mask, lower_p[r], 0.0).astype(BF16), spread(low[r])) for r in heads
        ]
        inverse = [inverse[r] - dot(low[r], spread(inner[r].astype(BF16))) for r in heads]
        width *= 2
    inverse = [
        jnp.where(same_block, jnp.concatenate([inverse[r]] * blocks, axis=0), 0.0) for r in heads
    ]
    @pl.when(jnp.logical_and(ready, odd))
    def _():
        forward(step - lag)

    while width < count:
        mask = (apart >= width) & (apart < 2 * width)
        low = [inverse[r].astype(BF16) for r in heads]
        inner = [dot(jnp.where(mask, lower[r], 0.0).astype(BF16), low[r]) for r in heads]
        inverse = [inverse[r] - dot(low[r], inner[r].astype(BF16)) for r in heads]
        width *= 2
    small = identity[:DK, :DK]
    grown = [jnp.exp(cum[r]) for r in heads]
    solved = []
    for r in heads:
        rhs = jnp.concatenate(
            [
                beta[r] * value[:, r * DK : (r + 1) * DK],
                (beta[r] * grown[r]) * keys[r // ratio],
            ],
            axis=1,
        )
        solved.append(dot2(inverse[r], rhs))
    for r in heads:
        head = step * group + r
        last = cum[r][count - 1 : count, :]
        faded = keys[r // ratio] * jnp.exp(last - cum[r])
        ahead = dot2(faded, solved[r], TN)
        out = dot1(scores[r // ratio] * fade[r], solved[r])
        base_ref[head, 0:DK, :] = ahead[:, :DK]
        base_ref[head, DK : DK + count, :] = out[:, :DK]
        mh, ml = pieces(jnp.exp(last) * small - ahead[:, DK:])
        map_high[head] = mh
        map_low[head] = ml
        reader[head] = (grown[r] * queries[r // ratio] - out[:, DK:]).astype(BF16)

    gain = gain_ref[...]

    def finish(p):
        for r in heads:
            h = p * group + r
            place = pl.ds(pl.multiple_of(h * DK, DK), DK)
            rows = dot(reader[h], entering[h]) + base_ref[h, DK : DK + count, :]
            mean = jnp.mean(rows * rows, axis=-1, keepdims=True)
            gate = gate_ref[:, place].astype(F32)
            out_ref[:, place] = (rows * lax.rsqrt(mean + 1e-06) * gain * silu(gate)).astype(BF16)

    @pl.when(jnp.logical_and(ready, jnp.logical_not(odd)))
    def _():
        forward(step - lag)

    @pl.when(step == steps - 1)
    def _():
        start = jnp.maximum(steps - lag, 0)

        @pl.loop(start, steps)
        def _(p):
            forward_each(p)
            finish(p)

        @pl.loop(0, start)
        def _(p):
            finish(p)

        @pl.when(has_right)
        def _():
            for h in range(total_heads):
                hop(h).wait_send()


def shards(
    query_proj, key_proj, value_proj, gate_proj, write_strength, log_decay,
    conv_query, conv_key, conv_value, norm_gain,
):
    n = lax.axis_size("seq")
    count = query_proj.shape[0]
    key_heads = query_proj.shape[1] // DK
    heads = write_strength.shape[1]
    ratio = heads // key_heads
    per_step = KEY_HEADS_A_STEP
    steps = key_heads // per_step
    taps = conv_query.shape[0]
    kw = per_step * DK
    vw = ratio * kw

    def col(height, w):
        return pl.BlockSpec((height, w), lambda i: (0, i))

    def whole(x):
        return pl.BlockSpec(x.shape, lambda i: (0, 0))

    def tail(x):
        return pl.BlockSpec((TILE, x.shape[1]), lambda i: (count // TILE - 1, 0))

    beta_t = write_strength.T
    decay_t = log_decay.T
    gain = norm_gain.reshape(1, -1)
    return pl.pallas_call(
        functools.partial(kernel, n, ratio, per_step, steps),
        grid=(steps,),
        in_specs=[
            tail(query_proj), tail(key_proj), tail(value_proj),
            col(count, kw), col(count, kw), col(count, vw), whole(beta_t), whole(decay_t),
            col(taps, kw), col(taps, kw), col(taps, vw), whole(gate_proj), whole(gain),
        ],
        out_specs=pl.BlockSpec(memory_space=pltpu.VMEM),
        out_shape=jax.ShapeDtypeStruct(gate_proj.shape, BF16),
        scratch_shapes=[
            pltpu.VMEM((TILE + count, kw), F32),
            pltpu.VMEM((TILE + count, kw), F32),
            pltpu.VMEM((TILE + count, vw), F32),
            pltpu.VMEM((count, heads), F32),
            pltpu.VMEM((heads, count), F32),
            pltpu.VMEM((count, heads), F32),
            pltpu.VMEM((heads, DK, DK), BF16),
            pltpu.VMEM((heads, DK, DK), BF16),
            pltpu.VMEM((heads, count, DK), BF16),
            pltpu.VMEM((heads, DK + count, DK), F32),
            pltpu.VMEM((TILE, query_proj.shape[1]), BF16),
            pltpu.VMEM((TILE, key_proj.shape[1]), BF16),
            pltpu.VMEM((TILE, value_proj.shape[1]), BF16),
            pltpu.VMEM((heads, DK, DK), BF16),
            pltpu.VMEM((heads, DK, DK), BF16),
            pltpu.SemaphoreType.DMA((heads,)),
            pltpu.SemaphoreType.DMA((heads,)),
            pltpu.SemaphoreType.DMA((3,)),
            pltpu.SemaphoreType.DMA((3,)),
        ],
        compiler_params=pltpu.CompilerParams(
            collective_id=0, has_side_effects=True, vmem_limit_bytes=56 * 2**20
        ),
        name="delta_layer",
    )(
        query_proj, key_proj, value_proj, query_proj, key_proj, value_proj, beta_t, decay_t,
        conv_query, conv_key, conv_value, gate_proj, gain,
    )


def solution(mesh):
    split = P(("groups", "seq"), "head")
    in_specs = (split,) * 6 + (P(None, "head"),) * 3 + (P(),)
    return jax.shard_map(shards, mesh=mesh, in_specs=in_specs, out_specs=split, check_vma=False)
```

```python
import functools

import jax
import jax.numpy as jnp
from jax import lax
from jax.experimental import pallas as pl
from jax.experimental.pallas import tpu as pltpu
from jax.sharding import PartitionSpec as P

DK = 128
TILE = 16
KEY_HEADS_A_STEP = 2
BLOCK = 64
F32 = jnp.float32
BF16 = jnp.bfloat16
NN = (((1,), (0,)), ((), ()))
NT = (((1,), (1,)), ((), ()))
TN = (((0,), (0,)), ((), ()))


def pieces(x):
    high = x.astype(BF16)
    return high, (x - high.astype(F32)).astype(BF16)


def dot(a, b, dims=NN):
    return lax.dot_general(a, b, dims, preferred_element_type=F32)


def dot3(a, b, dims=NN):
    ah, al = pieces(a)
    bh, bl = pieces(b)
    return dot(ah, bh, dims) + dot(ah, bl, dims) + dot(al, bh, dims)


def dot1(a, b, dims=NN):
    return dot(a.astype(BF16), b.astype(BF16), dims)


def silu(u):
    return u / (1.0 + jnp.exp(-u))


def dot2(a, b, dims=NN):
    bh, bl = pieces(b)
    a = a.astype(BF16)
    return dot(a, bh, dims) + dot(a, bl, dims)


def precise(a, b, dims):
    return lax.dot_general(
        a, b, dims, precision=lax.Precision.HIGHEST, preferred_element_type=F32
    )


def conv_silu(rows, rim, source_ref, taps_ref):
    count = source_ref.shape[0]
    rows[0:TILE, :] = rim.astype(F32)
    rows[TILE : TILE + count, :] = source_ref[...].astype(F32)
    taps = taps_ref[...].astype(F32)
    first = TILE - taps.shape[0] + 1
    total = taps[0:1] * rows[first : first + count, :]
    for j in range(1, taps.shape[0]):
        total = total + taps[j : j + 1] * rows[first + j : first + j + count, :]
    return silu(total).astype(BF16).astype(F32)


def unit(x):
    return x * lax.rsqrt(jnp.sum(x * x, axis=-1, keepdims=True) + 1e-06)


def kernel(
    n, ratio, per_step, steps,
    tail_q, tail_k, tail_v, q_ref, k_ref, v_ref, beta_t, decay_t, tq, tk, tv, gate_ref, gain_ref,
    out_ref,
    rows_q, rows_k, rows_v, cum_ref, cum_t_ref, beta_ref,
    map_high, map_low, reader, base_ref, rim_q, rim_k, rim_v, entering, leaving,
    mate_maps, mate_bases, own, send_sem, recv_sem, map_send, map_recv, base_send, base_recv,
    rim_send, rim_recv,
):
    step = pl.program_id(0)
    me = lax.axis_index("seq")
    has_left = me > 0
    has_right = me < n - 1
    left = lax.rem(me + n - 1, n)
    right = lax.rem(me + 1, n)
    count = q_ref.shape[0]
    group = ratio * per_step
    total_heads = group * steps
    heads = range(group)
    row = lax.broadcasted_iota(jnp.int32, (count, count), 0)
    column = lax.broadcasted_iota(jnp.int32, (count, count), 1)
    upto = row >= column
    apart = jnp.where(upto, row ^ column, 0)
    identity = (row == column).astype(F32)

    def rim_hop(i):
        source, target = ((tail_q, rim_q), (tail_k, rim_k), (tail_v, rim_v))[i]
        return pltpu.make_async_remote_copy(
            src_ref=source, dst_ref=target, send_sem=rim_send.at[i], recv_sem=rim_recv.at[i],
            device_id={"seq": right}, device_id_type=pl.DeviceIdType.MESH,
        )

    pair = me // 2
    second = me % 2 == 1
    first = jnp.logical_not(second)
    later = pair > 0

    def hop(source, target, h, sends, receives, device):
        return pltpu.make_async_remote_copy(
            src_ref=source.at[h], dst_ref=target.at[h],
            send_sem=sends.at[h], recv_sem=receives.at[h],
            device_id={"seq": device}, device_id_type=pl.DeviceIdType.MESH,
        )

    def mate_map(h):
        return hop(map_high, mate_maps, h, map_send, map_recv, right)

    def mate_base(h):
        return hop(leaving, mate_bases, h, base_send, base_recv, right)

    def to_first(h):
        return hop(leaving, entering, h, base_send, recv_sem, right)

    def to_second(h):
        return hop(leaving, entering, h, send_sem, recv_sem, lax.rem(me + 2, n))

    @pl.when(step == 0)
    def _():
        barrier = pltpu.get_barrier_semaphore()

        @pl.when(has_left)
        def _():
            pl.semaphore_signal(
                barrier, inc=1, device_id={"seq": left}, device_id_type=pl.DeviceIdType.MESH
            )

        @pl.when(jnp.logical_and(second, later))
        def _():
            pl.semaphore_signal(
                barrier, inc=1, device_id={"seq": lax.rem(me + n - 2, n)},
                device_id_type=pl.DeviceIdType.MESH,
            )

        @pl.when(jnp.logical_and(second, has_right))
        def _():
            pl.semaphore_wait(barrier, 2)

        @pl.when(first)
        def _():
            pl.semaphore_wait(barrier, 1)

        @pl.when(has_right)
        def _():
            for i in range(3):
                rim_hop(i).start()

        ones = upto.astype(F32)
        cum_ref[...] = precise(ones, decay_t[...], NT)
        cum_t_ref[...] = precise(decay_t[...], ones, NT)
        beta_ref[...] = precise(identity, beta_t[...], NT)

        @pl.when(jnp.logical_not(later))
        def _():
            entering[...] = jnp.zeros_like(entering)

        @pl.when(jnp.logical_not(has_left))
        def _():
            for ref in (rim_q, rim_k, rim_v):
                ref[...] = jnp.zeros_like(ref)

        @pl.when(has_left)
        def _():
            for i in range(3):
                rim_hop(i).wait_recv()

        @pl.when(has_right)
        def _():
            for i in range(3):
                rim_hop(i).wait_send()

    def rim_of(ref, w):
        return ref[:, pl.ds(pl.multiple_of(step * w, 128), w)]

    def await_state(h):
        @pl.when(later)
        def _():
            to_second(h).wait_recv()

        @pl.when(second)
        def _():
            mate_base(h).wait_recv()
            mate_map(h).wait_recv()

    def own_state(h):
        state = dot(mate_maps[h, 0:DK], entering[h]) + mate_bases[h].astype(F32)
        own[h] = state.astype(BF16)

    def step_state(h):
        state = own[h]
        new = dot(map_high[h], state) + dot(map_low[h], state) + base_ref[h, 0:DK, :]
        leaving[h] = new.astype(BF16)

    def send_state(h):
        to_second(h).start()
        to_first(h).start()

    def forward(p):
        for r in heads:
            await_state(p * group + r)
        for r in heads:
            own_state(p * group + r)

        @pl.when(has_right)
        def _():
            for r in heads:
                step_state(p * group + r)
            for r in heads:
                send_state(p * group + r)

    def forward_each(p):
        for r in heads:
            h = p * group + r
            await_state(h)

            @pl.when(first)
            def _():
                own[h] = entering[h]

            @pl.when(second)
            def _():
                own_state(h)

                @pl.when(has_right)
                def _():
                    step_state(h)
                    send_state(h)

    lag = 1 + (pair + 1) // 2
    odd = pair % 2 == 1
    ready = jnp.logical_and(second, step >= lag)

    kw = per_step * DK
    vw = group * DK
    query_all = conv_silu(rows_q, rim_of(rim_q, kw), q_ref, tq)
    key_all = conv_silu(rows_k, rim_of(rim_k, kw), k_ref, tk)
    value = conv_silu(rows_v, rim_of(rim_v, vw), v_ref, tv)
    queries = [unit(query_all[:, g * DK : (g + 1) * DK]) * (DK ** -0.5) for g in range(per_step)]
    keys = [unit(key_all[:, g * DK : (g + 1) * DK]) for g in range(per_step)]
    grams = [dot3(keys[g], keys[g], NT) for g in range(per_step)]
    scores = [dot3(queries[g], keys[g], NT) for g in range(per_step)]
    lane = lax.broadcasted_iota(jnp.int32, beta_ref.shape, 1)
    cum, beta, fade, lower = [], [], [], []
    for r in heads:
        head = step * group + r
        chosen = lane == head
        c = jnp.sum(jnp.where(chosen, cum_ref[...], 0.0), axis=1, keepdims=True)
        b = jnp.sum(jnp.where(chosen, beta_ref[...], 0.0), axis=1, keepdims=True)
        gap = c - cum_t_ref[pl.ds(head, 1), :]
        f = jnp.where(upto, jnp.exp(jnp.where(upto, gap, 0.0)), 0.0)
        cum.append(c)
        beta.append(b)
        fade.append(f)
        lower.append(b * grams[r // ratio] * f)
    blocks = count // BLOCK
    row_p = lax.broadcasted_iota(jnp.int32, (BLOCK, count), 0)
    lane_p = lax.broadcasted_iota(jnp.int32, (BLOCK, count), 1)
    apart_p = jnp.where(row_p >= lane_p % BLOCK, row_p ^ (lane_p % BLOCK), 0)
    eye_p = (row_p == lane_p % BLOCK).astype(F32)
    same_block = row // BLOCK == column // BLOCK
    keep = same_block.astype(F32).astype(BF16)

    def pack(x):
        packed = x[0:BLOCK, :]
        for b in range(1, blocks):
            packed = jnp.where(lane_p // BLOCK == b, x[b * BLOCK : (b + 1) * BLOCK, :], packed)
        return packed

    def spread(x):
        return jnp.concatenate([x] * blocks, axis=0) * keep

    lower_p = [pack(lower[r]) for r in heads]
    inverse = [eye_p - jnp.where(apart_p == 1, lower_p[r], 0.0) for r in heads]
    width = 2
    while width < BLOCK:
        mask = (apart_p >= width) & (apart_p < 2 * width)
        low = [inverse[r].astype(BF16) for r in heads]
        inner = [
            dot(jnp.where(mask, lower_p[r], 0.0).astype(BF16), spread(low[r])) for r in heads
        ]
        inverse = [inverse[r] - dot(low[r], spread(inner[r].astype(BF16))) for r in heads]
        width *= 2
    inverse = [
        jnp.where(same_block, jnp.concatenate([inverse[r]] * blocks, axis=0), 0.0) for r in heads
    ]
    @pl.when(jnp.logical_and(ready, odd))
    def _():
        forward(step - lag)

    while width < count:
        mask = (apart >= width) & (apart < 2 * width)
        low = [inverse[r].astype(BF16) for r in heads]
        inner = [dot(jnp.where(mask, lower[r], 0.0).astype(BF16), low[r]) for r in heads]
        inverse = [inverse[r] - dot(low[r], inner[r].astype(BF16)) for r in heads]
        width *= 2
    small = identity[:DK, :DK]
    grown = [jnp.exp(cum[r]) for r in heads]
    solved = []
    for r in heads:
        rhs = jnp.concatenate(
            [
                beta[r] * value[:, r * DK : (r + 1) * DK],
                (beta[r] * grown[r]) * keys[r // ratio],
            ],
            axis=1,
        )
        solved.append(dot2(inverse[r], rhs))
    for r in heads:
        head = step * group + r
        last = cum[r][count - 1 : count, :]
        faded = keys[r // ratio] * jnp.exp(last - cum[r])
        ahead = dot2(faded, solved[r], TN)
        out = dot1(scores[r // ratio] * fade[r], solved[r])
        base_ref[head, 0:DK, :] = ahead[:, :DK]
        base_ref[head, DK : DK + count, :] = out[:, :DK]
        mh, ml = pieces(jnp.exp(last) * small - ahead[:, DK:])
        map_high[head] = mh
        map_low[head] = ml
        reader[head] = (grown[r] * queries[r // ratio] - out[:, DK:]).astype(BF16)

    gain = gain_ref[...]

    def finish(p):
        for r in heads:
            h = p * group + r
            place = pl.ds(pl.multiple_of(h * DK, DK), DK)
            rows = dot(reader[h], own[h]) + base_ref[h, DK : DK + count, :]
            mean = jnp.mean(rows * rows, axis=-1, keepdims=True)
            gate = gate_ref[:, place].astype(F32)
            out_ref[:, place] = (rows * lax.rsqrt(mean + 1e-06) * gain * silu(gate)).astype(BF16)

    @pl.when(first)
    def _():
        for r in heads:
            head = step * group + r
            leaving[head] = base_ref[head, 0:DK, :].astype(BF16)
            mate_base(head).start()
        for r in heads:
            mate_map(step * group + r).start()

    @pl.when(jnp.logical_and(ready, jnp.logical_not(odd)))
    def _():
        forward(step - lag)

    @pl.when(step == steps - 1)
    def _():
        start = jnp.where(second, jnp.maximum(steps - lag, 0), 0)

        @pl.loop(start, steps)
        def _(p):
            forward_each(p)
            finish(p)

        @pl.loop(0, start)
        def _(p):
            finish(p)

        @pl.loop(0, total_heads)
        def _(h):
            @pl.when(first)
            def _():
                mate_base(h).wait_send()
                mate_map(h).wait_send()

            @pl.when(jnp.logical_and(second, has_right))
            def _():
                to_first(h).wait_send()
                to_second(h).wait_send()


def shards(
    query_proj, key_proj, value_proj, gate_proj, write_strength, log_decay,
    conv_query, conv_key, conv_value, norm_gain,
):
    n = lax.axis_size("seq")
    count = query_proj.shape[0]
    key_heads = query_proj.shape[1] // DK
    heads = write_strength.shape[1]
    ratio = heads // key_heads
    per_step = KEY_HEADS_A_STEP
    steps = key_heads // per_step
    taps = conv_query.shape[0]
    kw = per_step * DK
    vw = ratio * kw

    def col(height, w):
        return pl.BlockSpec((height, w), lambda i: (0, i))

    def whole(x):
        return pl.BlockSpec(x.shape, lambda i: (0, 0))

    def tail(x):
        return pl.BlockSpec((TILE, x.shape[1]), lambda i: (count // TILE - 1, 0))

    beta_t = write_strength.T
    decay_t = log_decay.T
    gain = norm_gain.reshape(1, -1)
    return pl.pallas_call(
        functools.partial(kernel, n, ratio, per_step, steps),
        grid=(steps,),
        in_specs=[
            tail(query_proj), tail(key_proj), tail(value_proj),
            col(count, kw), col(count, kw), col(count, vw), whole(beta_t), whole(decay_t),
            col(taps, kw), col(taps, kw), col(taps, vw), whole(gate_proj), whole(gain),
        ],
        out_specs=pl.BlockSpec(memory_space=pltpu.VMEM),
        out_shape=jax.ShapeDtypeStruct(gate_proj.shape, BF16),
        scratch_shapes=[
            pltpu.VMEM((TILE + count, kw), F32),
            pltpu.VMEM((TILE + count, kw), F32),
            pltpu.VMEM((TILE + count, vw), F32),
            pltpu.VMEM((count, heads), F32),
            pltpu.VMEM((heads, count), F32),
            pltpu.VMEM((count, heads), F32),
            pltpu.VMEM((heads, DK, DK), BF16),
            pltpu.VMEM((heads, DK, DK), BF16),
            pltpu.VMEM((heads, count, DK), BF16),
            pltpu.VMEM((heads, DK + count, DK), F32),
            pltpu.VMEM((TILE, query_proj.shape[1]), BF16),
            pltpu.VMEM((TILE, key_proj.shape[1]), BF16),
            pltpu.VMEM((TILE, value_proj.shape[1]), BF16),
            pltpu.VMEM((heads, DK, DK), BF16),
            pltpu.VMEM((heads, DK, DK), BF16),
            pltpu.VMEM((heads, DK, DK), BF16),
            pltpu.VMEM((heads, DK, DK), BF16),
            pltpu.VMEM((heads, DK, DK), BF16),
            pltpu.SemaphoreType.DMA((heads,)),
            pltpu.SemaphoreType.DMA((heads,)),
            pltpu.SemaphoreType.DMA((heads,)),
            pltpu.SemaphoreType.DMA((heads,)),
            pltpu.SemaphoreType.DMA((heads,)),
            pltpu.SemaphoreType.DMA((heads,)),
            pltpu.SemaphoreType.DMA((3,)),
            pltpu.SemaphoreType.DMA((3,)),
        ],
        compiler_params=pltpu.CompilerParams(
            collective_id=0, has_side_effects=True, vmem_limit_bytes=56 * 2**20
        ),
        name="delta_layer",
    )(
        query_proj, key_proj, value_proj, query_proj, key_proj, value_proj, beta_t, decay_t,
        conv_query, conv_key, conv_value, gate_proj, gain,
    )


def solution(mesh):
    split = P(("groups", "seq"), "head")
    in_specs = (split,) * 6 + (P(None, "head"),) * 3 + (P(),)
    return jax.shard_map(shards, mesh=mesh, in_specs=in_specs, out_specs=split, check_vma=False)
```

```python
import functools

import jax
import jax.numpy as jnp
from jax import lax
from jax.experimental import pallas as pl
from jax.experimental.pallas import tpu as pltpu
from jax.sharding import PartitionSpec as P

DK = 128
TILE = 16
KEY_HEADS_A_STEP = 1
BLOCK = 64
F32 = jnp.float32
BF16 = jnp.bfloat16
NN = (((1,), (0,)), ((), ()))
NT = (((1,), (1,)), ((), ()))
TN = (((0,), (0,)), ((), ()))


def pieces(x):
    high = x.astype(BF16)
    return high, (x - high.astype(F32)).astype(BF16)


def dot(a, b, dims=NN):
    return lax.dot_general(a, b, dims, preferred_element_type=F32)


def dot3(a, b, dims=NN):
    ah, al = pieces(a)
    bh, bl = pieces(b)
    return dot(ah, bh, dims) + dot(ah, bl, dims) + dot(al, bh, dims)


def dot1(a, b, dims=NN):
    return dot(a.astype(BF16), b.astype(BF16), dims)


def silu(u):
    return u / (1.0 + jnp.exp(-u))


def dot2(a, b, dims=NN):
    bh, bl = pieces(b)
    a = a.astype(BF16)
    return dot(a, bh, dims) + dot(a, bl, dims)


def precise(a, b, dims):
    return lax.dot_general(
        a, b, dims, precision=lax.Precision.HIGHEST, preferred_element_type=F32
    )


def conv_silu(rows, rim, source_ref, taps_ref):
    count = source_ref.shape[0]
    rows[0:TILE, :] = rim.astype(F32)
    rows[TILE : TILE + count, :] = source_ref[...].astype(F32)
    taps = taps_ref[...].astype(F32)
    first = TILE - taps.shape[0] + 1
    total = taps[0:1] * rows[first : first + count, :]
    for j in range(1, taps.shape[0]):
        total = total + taps[j : j + 1] * rows[first + j : first + j + count, :]
    return silu(total).astype(BF16).astype(F32)


def unit(x):
    return x * lax.rsqrt(jnp.sum(x * x, axis=-1, keepdims=True) + 1e-06)


def kernel(
    n, ratio, per_step, steps,
    tail_q, tail_k, tail_v, q_ref, k_ref, v_ref, beta_t, decay_t, tq, tk, tv, gate_ref, gain_ref,
    out_ref,
    rows_q, rows_k, rows_v, cum_ref, cum_t_ref, beta_ref,
    map_high, map_low, reader, base_ref, rim_q, rim_k, rim_v, entering, leaving,
    send_sem, recv_sem, rim_send, rim_recv,
):
    step = pl.program_id(0)
    me = lax.axis_index("seq")
    has_left = me > 0
    has_right = me < n - 1
    left = lax.rem(me + n - 1, n)
    right = lax.rem(me + 1, n)
    count = q_ref.shape[0]
    group = ratio * per_step
    total_heads = group * steps
    heads = range(group)
    row = lax.broadcasted_iota(jnp.int32, (count, count), 0)
    column = lax.broadcasted_iota(jnp.int32, (count, count), 1)
    upto = row >= column
    apart = jnp.where(upto, row ^ column, 0)
    identity = (row == column).astype(F32)

    def rim_hop(i):
        source, target = ((tail_q, rim_q), (tail_k, rim_k), (tail_v, rim_v))[i]
        return pltpu.make_async_remote_copy(
            src_ref=source, dst_ref=target, send_sem=rim_send.at[i], recv_sem=rim_recv.at[i],
            device_id={"seq": right}, device_id_type=pl.DeviceIdType.MESH,
        )

    def hop(h):
        return pltpu.make_async_remote_copy(
            src_ref=leaving.at[h], dst_ref=entering.at[h],
            send_sem=send_sem.at[h], recv_sem=recv_sem.at[h],
            device_id={"seq": right}, device_id_type=pl.DeviceIdType.MESH,
        )

    @pl.when(step == 0)
    def _():
        barrier = pltpu.get_barrier_semaphore()

        @pl.when(has_left)
        def _():
            pl.semaphore_signal(
                barrier, inc=1, device_id={"seq": left}, device_id_type=pl.DeviceIdType.MESH
            )

        @pl.when(has_right)
        def _():
            pl.semaphore_wait(barrier, 1)
            for i in range(3):
                rim_hop(i).start()

        ones = upto.astype(F32)
        cum_ref[...] = precise(ones, decay_t[...], NT)
        cum_t_ref[...] = precise(decay_t[...], ones, NT)
        beta_ref[...] = precise(identity, beta_t[...], NT)

        @pl.when(jnp.logical_not(has_left))
        def _():
            entering[...] = jnp.zeros_like(entering)
            for ref in (rim_q, rim_k, rim_v):
                ref[...] = jnp.zeros_like(ref)

        @pl.when(has_left)
        def _():
            for i in range(3):
                rim_hop(i).wait_recv()

        @pl.when(has_right)
        def _():
            for i in range(3):
                rim_hop(i).wait_send()

    def rim_of(ref, w):
        return ref[:, pl.ds(pl.multiple_of(step * w, 128), w)]

    def step_state(h):
        state = entering[h]
        new = dot(map_high[h], state) + dot(map_low[h], state) + base_ref[h, 0:DK, :]
        leaving[h] = new.astype(BF16)

    def forward(p):
        @pl.when(has_left)
        def _():
            for r in heads:
                hop(p * group + r).wait_recv()

        @pl.when(has_right)
        def _():
            for r in heads:
                step_state(p * group + r)
            for r in heads:
                hop(p * group + r).start()

    def forward_each(p):
        for r in heads:
            h = p * group + r

            @pl.when(has_left)
            def _():
                hop(h).wait_recv()

            @pl.when(has_right)
            def _():
                step_state(h)
                hop(h).start()

    lag = (me + 1) // 2
    odd = me % 2 == 1
    ready = step >= lag

    kw = per_step * DK
    vw = group * DK
    query_all = conv_silu(rows_q, rim_of(rim_q, kw), q_ref, tq)
    key_all = conv_silu(rows_k, rim_of(rim_k, kw), k_ref, tk)
    value = conv_silu(rows_v, rim_of(rim_v, vw), v_ref, tv)
    queries = [unit(query_all[:, g * DK : (g + 1) * DK]) * (DK ** -0.5) for g in range(per_step)]
    keys = [unit(key_all[:, g * DK : (g + 1) * DK]) for g in range(per_step)]
    grams = [dot3(keys[g], keys[g], NT) for g in range(per_step)]
    scores = [dot3(queries[g], keys[g], NT) for g in range(per_step)]
    lane = lax.broadcasted_iota(jnp.int32, beta_ref.shape, 1)
    cum, beta, fade, lower = [], [], [], []
    for r in heads:
        head = step * group + r
        chosen = lane == head
        c = jnp.sum(jnp.where(chosen, cum_ref[...], 0.0), axis=1, keepdims=True)
        b = jnp.sum(jnp.where(chosen, beta_ref[...], 0.0), axis=1, keepdims=True)
        gap = c - cum_t_ref[pl.ds(head, 1), :]
        f = jnp.where(upto, jnp.exp(jnp.where(upto, gap, 0.0)), 0.0)
        cum.append(c)
        beta.append(b)
        fade.append(f)
        lower.append(b * grams[r // ratio] * f)
    blocks = count // BLOCK
    row_p = lax.broadcasted_iota(jnp.int32, (BLOCK, count), 0)
    lane_p = lax.broadcasted_iota(jnp.int32, (BLOCK, count), 1)
    apart_p = jnp.where(row_p >= lane_p % BLOCK, row_p ^ (lane_p % BLOCK), 0)
    eye_p = (row_p == lane_p % BLOCK).astype(F32)
    same_block = row // BLOCK == column // BLOCK
    keep = same_block.astype(F32).astype(BF16)

    def pack(x):
        packed = x[0:BLOCK, :]
        for b in range(1, blocks):
            packed = jnp.where(lane_p // BLOCK == b, x[b * BLOCK : (b + 1) * BLOCK, :], packed)
        return packed

    def spread(x):
        return jnp.concatenate([x] * blocks, axis=0) * keep

    lower_p = [pack(lower[r]) for r in heads]
    inverse = [eye_p - jnp.where(apart_p == 1, lower_p[r], 0.0) for r in heads]
    width = 2
    while width < BLOCK:
        mask = (apart_p >= width) & (apart_p < 2 * width)
        low = [inverse[r].astype(BF16) for r in heads]
        inner = [
            dot(jnp.where(mask, lower_p[r], 0.0).astype(BF16), spread(low[r])) for r in heads
        ]
        inverse = [inverse[r] - dot(low[r], spread(inner[r].astype(BF16))) for r in heads]
        width *= 2
    inverse = [
        jnp.where(same_block, jnp.concatenate([inverse[r]] * blocks, axis=0), 0.0) for r in heads
    ]
    @pl.when(jnp.logical_and(ready, odd))
    def _():
        forward(step - lag)

    while width < count:
        mask = (apart >= width) & (apart < 2 * width)
        low = [inverse[r].astype(BF16) for r in heads]
        inner = [dot(jnp.where(mask, lower[r], 0.0).astype(BF16), low[r]) for r in heads]
        inverse = [inverse[r] - dot(low[r], inner[r].astype(BF16)) for r in heads]
        width *= 2
    small = identity[:DK, :DK]
    grown = [jnp.exp(cum[r]) for r in heads]
    solved = []
    for r in heads:
        rhs = jnp.concatenate(
            [
                beta[r] * value[:, r * DK : (r + 1) * DK],
                (beta[r] * grown[r]) * keys[r // ratio],
            ],
            axis=1,
        )
        solved.append(dot2(inverse[r], rhs))
    for r in heads:
        head = step * group + r
        last = cum[r][count - 1 : count, :]
        faded = keys[r // ratio] * jnp.exp(last - cum[r])
        ahead = dot2(faded, solved[r], TN)
        out = dot1(scores[r // ratio] * fade[r], solved[r])
        base_ref[head, 0:DK, :] = ahead[:, :DK]
        base_ref[head, DK : DK + count, :] = out[:, :DK]
        mh, ml = pieces(jnp.exp(last) * small - ahead[:, DK:])
        map_high[head] = mh
        map_low[head] = ml
        reader[head] = (grown[r] * queries[r // ratio] - out[:, DK:]).astype(BF16)

    gain = gain_ref[...]

    def finish(p):
        for r in heads:
            h = p * group + r
            place = pl.ds(pl.multiple_of(h * DK, DK), DK)
            rows = dot(reader[h], entering[h]) + base_ref[h, DK : DK + count, :]
            mean = jnp.mean(rows * rows, axis=-1, keepdims=True)
            gate = gate_ref[:, place].astype(F32)
            out_ref[:, place] = (rows * lax.rsqrt(mean + 1e-06) * gain * silu(gate)).astype(BF16)

    @pl.when(jnp.logical_and(ready, jnp.logical_not(odd)))
    def _():
        forward(step - lag)

    @pl.when(step == steps - 1)
    def _():
        start = jnp.maximum(steps - lag, 0)

        @pl.loop(start, steps)
        def _(p):
            forward_each(p)
            finish(p)

        @pl.loop(0, start)
        def _(p):
            finish(p)

        @pl.when(has_right)
        def _():
            for h in range(total_heads):
                hop(h).wait_send()


def shards(
    query_proj, key_proj, value_proj, gate_proj, write_strength, log_decay,
    conv_query, conv_key, conv_value, norm_gain,
):
    n = lax.axis_size("seq")
    count = query_proj.shape[0]
    key_heads = query_proj.shape[1] // DK
    heads = write_strength.shape[1]
    ratio = heads // key_heads
    per_step = KEY_HEADS_A_STEP
    steps = key_heads // per_step
    taps = conv_query.shape[0]
    kw = per_step * DK
    vw = ratio * kw

    def col(height, w):
        return pl.BlockSpec((height, w), lambda i: (0, i))

    def whole(x):
        return pl.BlockSpec(x.shape, lambda i: (0, 0))

    def tail(x):
        return pl.BlockSpec((TILE, x.shape[1]), lambda i: (count // TILE - 1, 0))

    beta_t = write_strength.T
    decay_t = log_decay.T
    gain = norm_gain.reshape(1, -1)
    return pl.pallas_call(
        functools.partial(kernel, n, ratio, per_step, steps),
        grid=(steps,),
        in_specs=[
            tail(query_proj), tail(key_proj), tail(value_proj),
            col(count, kw), col(count, kw), col(count, vw), whole(beta_t), whole(decay_t),
            col(taps, kw), col(taps, kw), col(taps, vw), whole(gate_proj), whole(gain),
        ],
        out_specs=pl.BlockSpec(memory_space=pltpu.VMEM),
        out_shape=jax.ShapeDtypeStruct(gate_proj.shape, BF16),
        scratch_shapes=[
            pltpu.VMEM((TILE + count, kw), F32),
            pltpu.VMEM((TILE + count, kw), F32),
            pltpu.VMEM((TILE + count, vw), F32),
            pltpu.VMEM((count, heads), F32),
            pltpu.VMEM((heads, count), F32),
            pltpu.VMEM((count, heads), F32),
            pltpu.VMEM((heads, DK, DK), BF16),
            pltpu.VMEM((heads, DK, DK), BF16),
            pltpu.VMEM((heads, count, DK), BF16),
            pltpu.VMEM((heads, DK + count, DK), F32),
            pltpu.VMEM((TILE, query_proj.shape[1]), BF16),
            pltpu.VMEM((TILE, key_proj.shape[1]), BF16),
            pltpu.VMEM((TILE, value_proj.shape[1]), BF16),
            pltpu.VMEM((heads, DK, DK), BF16),
            pltpu.VMEM((heads, DK, DK), BF16),
            pltpu.SemaphoreType.DMA((heads,)),
            pltpu.SemaphoreType.DMA((heads,)),
            pltpu.SemaphoreType.DMA((3,)),
            pltpu.SemaphoreType.DMA((3,)),
        ],
        compiler_params=pltpu.CompilerParams(
            collective_id=0, has_side_effects=True, vmem_limit_bytes=56 * 2**20
        ),
        name="delta_layer",
    )(
        query_proj, key_proj, value_proj, query_proj, key_proj, value_proj, beta_t, decay_t,
        conv_query, conv_key, conv_value, gate_proj, gain,
    )


def solution(mesh):
    split = P(("groups", "seq"), "head")
    in_specs = (split,) * 6 + (P(None, "head"),) * 3 + (P(),)
    return jax.shard_map(shards, mesh=mesh, in_specs=in_specs, out_specs=split, check_vma=False)
```

```python
import functools

import jax
import jax.numpy as jnp
from jax import lax
from jax.experimental import pallas as pl
from jax.experimental.pallas import tpu as pltpu
from jax.sharding import PartitionSpec as P

DK = 128
TILE = 16
KEY_HEADS_A_STEP = 4
BLOCK = 64
F32 = jnp.float32
BF16 = jnp.bfloat16
NN = (((1,), (0,)), ((), ()))
NT = (((1,), (1,)), ((), ()))
TN = (((0,), (0,)), ((), ()))


def pieces(x):
    high = x.astype(BF16)
    return high, (x - high.astype(F32)).astype(BF16)


def dot(a, b, dims=NN):
    return lax.dot_general(a, b, dims, preferred_element_type=F32)


def dot3(a, b, dims=NN):
    ah, al = pieces(a)
    bh, bl = pieces(b)
    return dot(ah, bh, dims) + dot(ah, bl, dims) + dot(al, bh, dims)


def dot1(a, b, dims=NN):
    return dot(a.astype(BF16), b.astype(BF16), dims)


def silu(u):
    return u / (1.0 + jnp.exp(-u))


def dot2(a, b, dims=NN):
    bh, bl = pieces(b)
    a = a.astype(BF16)
    return dot(a, bh, dims) + dot(a, bl, dims)


def precise(a, b, dims):
    return lax.dot_general(
        a, b, dims, precision=lax.Precision.HIGHEST, preferred_element_type=F32
    )


def conv_silu(rows, rim, source_ref, taps_ref):
    count = source_ref.shape[0]
    rows[0:TILE, :] = rim.astype(F32)
    rows[TILE : TILE + count, :] = source_ref[...].astype(F32)
    taps = taps_ref[...].astype(F32)
    first = TILE - taps.shape[0] + 1
    total = taps[0:1] * rows[first : first + count, :]
    for j in range(1, taps.shape[0]):
        total = total + taps[j : j + 1] * rows[first + j : first + j + count, :]
    return silu(total).astype(BF16).astype(F32)


def unit(x):
    return x * lax.rsqrt(jnp.sum(x * x, axis=-1, keepdims=True) + 1e-06)


def kernel(
    n, ratio, per_step, steps,
    tail_q, tail_k, tail_v, q_ref, k_ref, v_ref, beta_t, decay_t, tq, tk, tv, gate_ref, gain_ref,
    out_ref,
    rows_q, rows_k, rows_v, cum_ref, cum_t_ref, beta_ref,
    map_high, map_low, reader, base_ref, rim_q, rim_k, rim_v, entering, leaving,
    send_sem, recv_sem, rim_send, rim_recv,
):
    step = pl.program_id(0)
    me = lax.axis_index("seq")
    has_left = me > 0
    has_right = me < n - 1
    left = lax.rem(me + n - 1, n)
    right = lax.rem(me + 1, n)
    count = q_ref.shape[0]
    group = ratio * per_step
    total_heads = group * steps
    heads = range(group)
    row = lax.broadcasted_iota(jnp.int32, (count, count), 0)
    column = lax.broadcasted_iota(jnp.int32, (count, count), 1)
    upto = row >= column
    apart = jnp.where(upto, row ^ column, 0)
    identity = (row == column).astype(F32)

    def rim_hop(i):
        source, target = ((tail_q, rim_q), (tail_k, rim_k), (tail_v, rim_v))[i]
        return pltpu.make_async_remote_copy(
            src_ref=source, dst_ref=target, send_sem=rim_send.at[i], recv_sem=rim_recv.at[i],
            device_id={"seq": right}, device_id_type=pl.DeviceIdType.MESH,
        )

    def hop(h):
        return pltpu.make_async_remote_copy(
            src_ref=leaving.at[h], dst_ref=entering.at[h],
            send_sem=send_sem.at[h], recv_sem=recv_sem.at[h],
            device_id={"seq": right}, device_id_type=pl.DeviceIdType.MESH,
        )

    @pl.when(step == 0)
    def _():
        barrier = pltpu.get_barrier_semaphore()

        @pl.when(has_left)
        def _():
            pl.semaphore_signal(
                barrier, inc=1, device_id={"seq": left}, device_id_type=pl.DeviceIdType.MESH
            )

        @pl.when(has_right)
        def _():
            pl.semaphore_wait(barrier, 1)
            for i in range(3):
                rim_hop(i).start()

        ones = upto.astype(F32)
        cum_ref[...] = precise(ones, decay_t[...], NT)
        cum_t_ref[...] = precise(decay_t[...], ones, NT)
        beta_ref[...] = precise(identity, beta_t[...], NT)

        @pl.when(jnp.logical_not(has_left))
        def _():
            entering[...] = jnp.zeros_like(entering)
            for ref in (rim_q, rim_k, rim_v):
                ref[...] = jnp.zeros_like(ref)

        @pl.when(has_left)
        def _():
            for i in range(3):
                rim_hop(i).wait_recv()

        @pl.when(has_right)
        def _():
            for i in range(3):
                rim_hop(i).wait_send()

    def rim_of(ref, w):
        return ref[:, pl.ds(pl.multiple_of(step * w, 128), w)]

    def step_state(h):
        state = entering[h]
        new = dot(map_high[h], state) + dot(map_low[h], state) + base_ref[h, 0:DK, :]
        leaving[h] = new.astype(BF16)

    def forward(p):
        @pl.when(has_left)
        def _():
            for r in heads:
                hop(p * group + r).wait_recv()

        @pl.when(has_right)
        def _():
            for r in heads:
                step_state(p * group + r)
            for r in heads:
                hop(p * group + r).start()

    def forward_each(p):
        for r in heads:
            h = p * group + r

            @pl.when(has_left)
            def _():
                hop(h).wait_recv()

            @pl.when(has_right)
            def _():
                step_state(h)
                hop(h).start()

    lag = (me + 1) // 2
    odd = me % 2 == 1
    ready = step >= lag

    kw = per_step * DK
    vw = group * DK
    query_all = conv_silu(rows_q, rim_of(rim_q, kw), q_ref, tq)
    key_all = conv_silu(rows_k, rim_of(rim_k, kw), k_ref, tk)
    value = conv_silu(rows_v, rim_of(rim_v, vw), v_ref, tv)
    queries = [unit(query_all[:, g * DK : (g + 1) * DK]) * (DK ** -0.5) for g in range(per_step)]
    keys = [unit(key_all[:, g * DK : (g + 1) * DK]) for g in range(per_step)]
    grams = [dot3(keys[g], keys[g], NT) for g in range(per_step)]
    scores = [dot3(queries[g], keys[g], NT) for g in range(per_step)]
    lane = lax.broadcasted_iota(jnp.int32, beta_ref.shape, 1)
    cum, beta, fade, lower = [], [], [], []
    for r in heads:
        head = step * group + r
        chosen = lane == head
        c = jnp.sum(jnp.where(chosen, cum_ref[...], 0.0), axis=1, keepdims=True)
        b = jnp.sum(jnp.where(chosen, beta_ref[...], 0.0), axis=1, keepdims=True)
        gap = c - cum_t_ref[pl.ds(head, 1), :]
        f = jnp.where(upto, jnp.exp(jnp.where(upto, gap, 0.0)), 0.0)
        cum.append(c)
        beta.append(b)
        fade.append(f)
        lower.append(b * grams[r // ratio] * f)
    blocks = count // BLOCK
    row_p = lax.broadcasted_iota(jnp.int32, (BLOCK, count), 0)
    lane_p = lax.broadcasted_iota(jnp.int32, (BLOCK, count), 1)
    apart_p = jnp.where(row_p >= lane_p % BLOCK, row_p ^ (lane_p % BLOCK), 0)
    eye_p = (row_p == lane_p % BLOCK).astype(F32)
    same_block = row // BLOCK == column // BLOCK
    keep = same_block.astype(F32).astype(BF16)

    def pack(x):
        packed = x[0:BLOCK, :]
        for b in range(1, blocks):
            packed = jnp.where(lane_p // BLOCK == b, x[b * BLOCK : (b + 1) * BLOCK, :], packed)
        return packed

    def spread(x):
        return jnp.concatenate([x] * blocks, axis=0) * keep

    lower_p = [pack(lower[r]) for r in heads]
    inverse = [eye_p - jnp.where(apart_p == 1, lower_p[r], 0.0) for r in heads]
    width = 2
    while width < BLOCK:
        mask = (apart_p >= width) & (apart_p < 2 * width)
        low = [inverse[r].astype(BF16) for r in heads]
        inner = [
            dot(jnp.where(mask, lower_p[r], 0.0).astype(BF16), spread(low[r])) for r in heads
        ]
        inverse = [inverse[r] - dot(low[r], spread(inner[r].astype(BF16))) for r in heads]
        width *= 2
    inverse = [
        jnp.where(same_block, jnp.concatenate([inverse[r]] * blocks, axis=0), 0.0) for r in heads
    ]
    @pl.when(jnp.logical_and(ready, odd))
    def _():
        forward(step - lag)

    while width < count:
        mask = (apart >= width) & (apart < 2 * width)
        low = [inverse[r].astype(BF16) for r in heads]
        inner = [dot(jnp.where(mask, lower[r], 0.0).astype(BF16), low[r]) for r in heads]
        inverse = [inverse[r] - dot(low[r], inner[r].astype(BF16)) for r in heads]
        width *= 2
    small = identity[:DK, :DK]
    grown = [jnp.exp(cum[r]) for r in heads]
    solved = []
    for r in heads:
        rhs = jnp.concatenate(
            [
                beta[r] * value[:, r * DK : (r + 1) * DK],
                (beta[r] * grown[r]) * keys[r // ratio],
            ],
            axis=1,
        )
        solved.append(dot2(inverse[r], rhs))
    for r in heads:
        head = step * group + r
        last = cum[r][count - 1 : count, :]
        faded = keys[r // ratio] * jnp.exp(last - cum[r])
        ahead = dot2(faded, solved[r], TN)
        out = dot1(scores[r // ratio] * fade[r], solved[r])
        base_ref[head, 0:DK, :] = ahead[:, :DK]
        base_ref[head, DK : DK + count, :] = out[:, :DK]
        mh, ml = pieces(jnp.exp(last) * small - ahead[:, DK:])
        map_high[head] = mh
        map_low[head] = ml
        reader[head] = (grown[r] * queries[r // ratio] - out[:, DK:]).astype(BF16)

    gain = gain_ref[...]

    def finish(p):
        for r in heads:
            h = p * group + r
            place = pl.ds(pl.multiple_of(h * DK, DK), DK)
            rows = dot(reader[h], entering[h]) + base_ref[h, DK : DK + count, :]
            mean = jnp.mean(rows * rows, axis=-1, keepdims=True)
            gate = gate_ref[:, place].astype(F32)
            out_ref[:, place] = (rows * lax.rsqrt(mean + 1e-06) * gain * silu(gate)).astype(BF16)

    @pl.when(jnp.logical_and(ready, jnp.logical_not(odd)))
    def _():
        forward(step - lag)

    @pl.when(step == steps - 1)
    def _():
        start = jnp.maximum(steps - lag, 0)

        @pl.loop(start, steps)
        def _(p):
            forward_each(p)
            finish(p)

        @pl.loop(0, start)
        def _(p):
            finish(p)

        @pl.when(has_right)
        def _():
            for h in range(total_heads):
                hop(h).wait_send()


def shards(
    query_proj, key_proj, value_proj, gate_proj, write_strength, log_decay,
    conv_query, conv_key, conv_value, norm_gain,
):
    n = lax.axis_size("seq")
    count = query_proj.shape[0]
    key_heads = query_proj.shape[1] // DK
    heads = write_strength.shape[1]
    ratio = heads // key_heads
    per_step = KEY_HEADS_A_STEP
    steps = key_heads // per_step
    taps = conv_query.shape[0]
    kw = per_step * DK
    vw = ratio * kw

    def col(height, w):
        return pl.BlockSpec((height, w), lambda i: (0, i))

    def whole(x):
        return pl.BlockSpec(x.shape, lambda i: (0, 0))

    def tail(x):
        return pl.BlockSpec((TILE, x.shape[1]), lambda i: (count // TILE - 1, 0))

    beta_t = write_strength.T
    decay_t = log_decay.T
    gain = norm_gain.reshape(1, -1)
    return pl.pallas_call(
        functools.partial(kernel, n, ratio, per_step, steps),
        grid=(steps,),
        in_specs=[
            tail(query_proj), tail(key_proj), tail(value_proj),
            col(count, kw), col(count, kw), col(count, vw), whole(beta_t), whole(decay_t),
            col(taps, kw), col(taps, kw), col(taps, vw), whole(gate_proj), whole(gain),
        ],
        out_specs=pl.BlockSpec(memory_space=pltpu.VMEM),
        out_shape=jax.ShapeDtypeStruct(gate_proj.shape, BF16),
        scratch_shapes=[
            pltpu.VMEM((TILE + count, kw), F32),
            pltpu.VMEM((TILE + count, kw), F32),
            pltpu.VMEM((TILE + count, vw), F32),
            pltpu.VMEM((count, heads), F32),
            pltpu.VMEM((heads, count), F32),
            pltpu.VMEM((count, heads), F32),
            pltpu.VMEM((heads, DK, DK), BF16),
            pltpu.VMEM((heads, DK, DK), BF16),
            pltpu.VMEM((heads, count, DK), BF16),
            pltpu.VMEM((heads, DK + count, DK), F32),
            pltpu.VMEM((TILE, query_proj.shape[1]), BF16),
            pltpu.VMEM((TILE, key_proj.shape[1]), BF16),
            pltpu.VMEM((TILE, value_proj.shape[1]), BF16),
            pltpu.VMEM((heads, DK, DK), BF16),
            pltpu.VMEM((heads, DK, DK), BF16),
            pltpu.SemaphoreType.DMA((heads,)),
            pltpu.SemaphoreType.DMA((heads,)),
            pltpu.SemaphoreType.DMA((3,)),
            pltpu.SemaphoreType.DMA((3,)),
        ],
        compiler_params=pltpu.CompilerParams(
            collective_id=0, has_side_effects=True, vmem_limit_bytes=56 * 2**20
        ),
        name="delta_layer",
    )(
        query_proj, key_proj, value_proj, query_proj, key_proj, value_proj, beta_t, decay_t,
        conv_query, conv_key, conv_value, gate_proj, gain,
    )


def solution(mesh):
    split = P(("groups", "seq"), "head")
    in_specs = (split,) * 6 + (P(None, "head"),) * 3 + (P(),)
    return jax.shard_map(shards, mesh=mesh, in_specs=in_specs, out_specs=split, check_vma=False)
```
